32 devices in a mesh: dp: 4 (over y, x), expert: 8 (over z, core).
Axes of the slice: x: 2, y: 2, z: 4, core: 2. Of those that a mesh axis runs over, the one named last changes fastest.
Arguments:
- tokens: bfloat16 [4096, 512], P(('dp', 'expert')), may hold values from -6 to 6
- codes: int32 [4096, 2], P(('dp', 'expert')), may hold values from 0 to 7, as said below
- cotangent: bfloat16 [4096, 512], P(('dp', 'expert')), may hold values from -6 to 6
- w_gate: bfloat16 [8, 512, 1024], P('expert'), may hold values from -0.25 to 0.25
- w_up: bfloat16 [8, 512, 1024], P('expert'), may hold values from -0.25 to 0.25
- w_down: bfloat16 [8, 1024, 512], P('expert'), may hold values from -0.1875 to 0.1875
Outputs:
- head_output: bfloat16 [4096, 512], P(('dp', 'expert'))
- grad_tokens: bfloat16 [4096, 512], P(('dp', 'expert'))
- grad_gate: bfloat16 [8, 512, 1024], P('expert', None, 'dp')
- grad_up: bfloat16 [8, 512, 1024], P('expert', None, 'dp')
- grad_down: bfloat16 [8, 1024, 512], P('expert', 'dp')
The draws below stay inside these ranges and needn't reach their ends.
Inputs may be any that keep to these rules, and one draw needn't show every extreme that they name: A token's two codes differ. Within each device's 128 tokens (aligned blocks of 128 rows), each arm is named at most 64 times over both columns, and one arm, the same for every block, is named exactly 64 times in every block.
All inputs are finite; a program needn't handle non-finite values.
Results may differ from the reference program's by a relative error of at most 0.009.
Values may be sent and summed in bfloat16 or wider, within the bound.
No kernel may reach another device: no remote copies, remote signals or barrier semaphores. Data moves between devices by JAX's collectives and lax.ppermute only.
A program may use at most 64 MiB of HBM per device.

```python
import jax
import jax.numpy as jnp
from jax import lax

DW = 512
HW = 1024
TOK_DEV = 128
E = 8
CAP = 64
TOKENS = 4096
N_DP = 4
N_EXPERT = 8


def draw_codes(key, part):
    block_count = TOKENS // TOK_DEV
    hot_arm = jax.random.randint(jax.random.fold_in(key, 7), (), 0, E).astype(jnp.int32)
    other_slots = (E - 1) * CAP
    picked_count = 2 * TOK_DEV - CAP

    def one_block(block_key):
        sub_keys = jax.random.split(block_key, 4)
        slot_order = jax.random.permutation(sub_keys[0], other_slots)
        chosen = slot_order < picked_count
        picked = jnp.nonzero(chosen, size=picked_count)[0]
        inner_ids = jnp.concatenate([jnp.zeros((CAP,), jnp.int32), (picked // CAP + 1).astype(jnp.int32)])
        others = (hot_arm + 1 + jax.random.permutation(sub_keys[1], E - 1).astype(jnp.int32)) % E
        labels = jnp.concatenate([hot_arm[None], others]).astype(jnp.int32)
        arm_list = labels[inner_ids]
        code_pairs = jnp.stack([arm_list[:TOK_DEV], arm_list[TOK_DEV:]], axis=1)
        swap_bits = jax.random.randint(sub_keys[2], (TOK_DEV, 1), 0, 2)
        code_pairs = jnp.where(swap_bits == 1, code_pairs[:, ::-1], code_pairs)
        shuffle = jax.random.permutation(sub_keys[3], TOK_DEV)
        return code_pairs[shuffle]
    block_keys = jax.vmap(lambda block_index: jax.random.fold_in(key, block_index))(jnp.arange(block_count))
    return jax.vmap(one_block)(block_keys).reshape(TOKENS, 2).astype(jnp.int32)


def block_scale(key, extent, pieces, smallest, high):
    def one(dim, shards_of):
        draws = jax.random.uniform(jax.random.fold_in(jax.random.fold_in(key, 6), dim), (shards_of,), jnp.float32, smallest / len(pieces), high / len(pieces))
        return jnp.repeat(jnp.exp(draws), extent[dim] // shards_of).reshape((-1,) + (1,) * (len(extent) - dim - 1))

    factor_of = one(*pieces[0])
    for cut in pieces[1:]:
        factor_of = factor_of * one(*cut)
    return factor_of


def scatter_about(key, shape, spread, bound, cuts=(), kind=jnp.bfloat16):
    values = spread * jax.random.normal(key, shape, jnp.float32)
    if cuts:
        values = values * block_scale(key, shape, cuts, -0.22, 0.18)
    return jnp.clip(values, -bound, bound).astype(kind)


def setup_inputs(seed: int = 0) -> dict:
    keys = jax.random.split(jax.random.key(seed), 7)
    return {
        "tokens": scatter_about(keys[0], (TOKENS, DW), 1.0, 6.0, ((0, 32),)),
        "codes": draw_codes(jax.random.fold_in(keys[6], 71), 0),
        "cotangent": scatter_about(keys[2], (TOKENS, DW), 1.0, 6.0, ((0, 32),)),
        "w_gate": scatter_about(keys[3], (E, DW, HW), DW ** -0.5, 0.25, ((0, 8),)),
        "w_up": scatter_about(keys[4], (E, DW, HW), DW ** -0.5, 0.25, ((0, 8),)),
        "w_down": scatter_about(keys[5], (E, HW, DW), HW ** -0.5, 0.1875, ((0, 8),)),
    }


fact_share = 0.7
counter_share = 0.3


def rounded(value):
    return lax.optimization_barrier(value.astype(jnp.bfloat16)).astype(jnp.float32)


def arm_pass(operands):
    arm_tokens, arm_cot, gate_w, up_w, down_w = operands
    tok_f = arm_tokens.astype(jnp.float32)
    cot_f = arm_cot.astype(jnp.float32)
    gate_f = gate_w.astype(jnp.float32)
    up_f = up_w.astype(jnp.float32)
    down_f = down_w.astype(jnp.float32)
    gate_pre = jnp.einsum("prc,ch->prh", tok_f, gate_f)
    up_pre = jnp.einsum("prc,ch->prh", tok_f, up_f)
    sigmoid_gate = jax.nn.sigmoid(gate_pre)
    activated = gate_pre * sigmoid_gate
    hidden = (activated * up_pre).astype(jnp.bfloat16)
    hidden_f = hidden.astype(jnp.float32)
    out_rows = jnp.einsum("prh,hc->prc", hidden_f, down_f).astype(jnp.bfloat16)
    d_hidden = jnp.einsum("prc,hc->prh", cot_f, down_f)
    d_up = (d_hidden * activated).astype(jnp.bfloat16).astype(jnp.float32)
    silu_slope = sigmoid_gate * (1.0 + gate_pre * (1.0 - sigmoid_gate))
    d_gate = (d_hidden * up_pre * silu_slope).astype(jnp.bfloat16).astype(jnp.float32)
    input_rows = (jnp.einsum("prh,ch->prc", d_gate, gate_f) + jnp.einsum("prh,ch->prc", d_up, up_f)).astype(jnp.bfloat16)
    grad_gate = jnp.sum(rounded(jnp.einsum("prc,prh->pch", tok_f, d_gate)), axis=0).astype(jnp.bfloat16)
    grad_up = jnp.sum(rounded(jnp.einsum("prc,prh->pch", tok_f, d_up)), axis=0).astype(jnp.bfloat16)
    grad_down = jnp.sum(rounded(jnp.einsum("prh,prc->phc", hidden_f, cot_f)), axis=0).astype(jnp.bfloat16)
    return out_rows, input_rows, grad_gate, grad_up, grad_down


def reference(tokens, codes, cotangent, w_gate, w_up, w_down):
    block_count = TOKENS // TOK_DEV
    flat_codes = codes.reshape(block_count, 2 * TOK_DEV).astype(jnp.int32)
    arm_ids = jnp.arange(E, dtype=jnp.int32)
    onehot = (flat_codes[:, :, None] == arm_ids[None, None, :]).astype(jnp.int32)
    earlier = jnp.cumsum(onehot, axis=1) - onehot
    destination = (flat_codes * CAP + jnp.sum(earlier * onehot, axis=2)).astype(jnp.int32)
    shares = jnp.tile(jnp.array([fact_share, counter_share], jnp.float32), TOK_DEV)
    token_rows = jnp.repeat(tokens.reshape(block_count, TOK_DEV, DW), 2, axis=1)
    cot_rows = (jnp.repeat(cotangent.reshape(block_count, TOK_DEV, DW).astype(jnp.float32), 2, axis=1) * shares[None, :, None]).astype(jnp.bfloat16)

    def place_rows(rows_in, where_to):
        return jnp.zeros((E * CAP, DW), jnp.bfloat16).at[where_to].set(rows_in)

    def arm_major(sent):
        return sent.reshape(N_DP, N_EXPERT, E, CAP, DW).transpose(2, 0, 1, 3, 4).reshape(E, N_DP, N_EXPERT * CAP, DW)

    def block_major(done):
        return done.reshape(E, N_DP, N_EXPERT, CAP, DW).transpose(1, 2, 0, 3, 4).reshape(block_count, E * CAP, DW)

    sent_tokens = arm_major(jax.vmap(place_rows)(token_rows, destination))
    sent_cot = arm_major(jax.vmap(place_rows)(cot_rows, destination))
    out_rows, input_rows, grad_gate, grad_up, grad_down = lax.map(arm_pass, (sent_tokens, sent_cot, w_gate, w_up, w_down))

    def pick_rows(table, where_to):
        return table[where_to]

    back_out = jax.vmap(pick_rows)(block_major(out_rows), destination).reshape(TOKENS, 2, DW).astype(jnp.float32)
    back_input = jax.vmap(pick_rows)(block_major(input_rows), destination).reshape(TOKENS, 2, DW).astype(jnp.float32)
    head_output = (fact_share * back_out[:, 0] + counter_share * back_out[:, 1]).astype(jnp.bfloat16)
    grad_tokens = (back_input[:, 0] + back_input[:, 1]).astype(jnp.bfloat16)
    return (head_output, grad_tokens, grad_gate, grad_up, grad_down)
```

```python
import functools

import jax
import jax.numpy as jnp
from jax import lax
from jax.experimental import pallas as pl
from jax.experimental.pallas import tpu as pltpu
from jax.sharding import PartitionSpec as P

fact_share = 0.7
counter_share = 0.3

F32 = jnp.float32
BF16 = jnp.bfloat16
CODE_ROWS = 16
VMEM_BYTES = 32 * 1024 * 1024

def rounded(value):
    return lax.optimization_barrier(value.astype(jnp.bfloat16)).astype(jnp.float32)


def silu_parts(gate_pre):
    sigmoid_gate = jax.nn.sigmoid(gate_pre)
    return (gate_pre * sigmoid_gate, sigmoid_gate * (1.0 + gate_pre * (1.0 - sigmoid_gate)))


def arm_forward(rows_in, gate_w, up_w):
    gate_pre = jnp.einsum("arc,ach->arh", rows_in, gate_w, preferred_element_type=jnp.float32)
    up_pre = jnp.einsum("arc,ach->arh", rows_in, up_w, preferred_element_type=jnp.float32)
    activated, silu_slope = silu_parts(gate_pre)
    hidden = (activated * up_pre).astype(jnp.bfloat16)
    return (up_pre, activated, silu_slope, hidden)


def arm_backward(up_pre, activated, silu_slope, cot_in, down_w):
    d_hidden = jnp.einsum("arc,ahc->arh", cot_in, down_w, preferred_element_type=jnp.float32)
    d_up = (d_hidden * activated).astype(jnp.bfloat16)
    d_gate = (d_hidden * up_pre * silu_slope).astype(jnp.bfloat16)
    return (d_gate, d_up)


def on_device(tokens, codes, cotangent, w_gate, w_up, w_down):
    token_count, feature_width = tokens.shape
    local_arms = w_gate.shape[0]
    arm_count = local_arms * lax.axis_size("expert")
    capacity = 4 * token_count // arm_count
    flat_codes = codes.reshape(-1)
    arm_ids = jnp.arange(arm_count, dtype=jnp.int32)
    onehot = (flat_codes[:, None] == arm_ids[None, :]).astype(jnp.int32)
    earlier = jnp.cumsum(onehot, axis=0) - onehot
    destination = flat_codes * capacity + jnp.sum(earlier * onehot, axis=1)
    shares = jnp.tile(jnp.array([fact_share, counter_share], jnp.float32), token_count)
    token_rows = jnp.repeat(tokens, 2, axis=0)
    cot_rows = (jnp.repeat(cotangent.astype(jnp.float32), 2, axis=0) * shares[:, None]).astype(
        jnp.bfloat16
    )
    blank_rows = jnp.zeros((arm_count * capacity, feature_width), jnp.bfloat16)
    send_tokens = (
        blank_rows.at[destination].set(token_rows).reshape(arm_count, capacity, feature_width)
    )
    send_cot = blank_rows.at[destination].set(cot_rows).reshape(arm_count, capacity, feature_width)
    arm_tokens, arm_cot = (
        lax.all_to_all(send_tokens, "expert", split_axis=0, concat_axis=1, tiled=True),
        lax.all_to_all(send_cot, "expert", split_axis=0, concat_axis=1, tiled=True),
    )
    up_pre, activated, silu_slope, hidden = arm_forward(arm_tokens, w_gate, w_up)
    out_rows = jnp.einsum(
        "arh,ahc->arc", hidden, w_down, preferred_element_type=jnp.float32
    ).astype(jnp.bfloat16)
    d_gate, d_up = arm_backward(up_pre, activated, silu_slope, arm_cot, w_down)
    input_rows = (
        jnp.einsum("arh,ach->arc", d_gate, w_gate, preferred_element_type=jnp.float32)
        + jnp.einsum("arh,ach->arc", d_up, w_up, preferred_element_type=jnp.float32)
    ).astype(jnp.bfloat16)
    back_out, back_input = (
        lax.all_to_all(out_rows, "expert", split_axis=1, concat_axis=0, tiled=True),
        lax.all_to_all(input_rows, "expert", split_axis=1, concat_axis=0, tiled=True),
    )
    back_out = back_out.reshape(arm_count * capacity, feature_width)[destination]
    back_out = back_out.reshape(token_count, 2, feature_width).astype(jnp.float32)
    back_input = back_input.reshape(arm_count * capacity, feature_width)[destination]
    back_input = back_input.reshape(token_count, 2, feature_width).astype(jnp.float32)
    head_output = (fact_share * back_out[:, 0] + counter_share * back_out[:, 1]).astype(
        jnp.bfloat16
    )
    grad_tokens = (back_input[:, 0] + back_input[:, 1]).astype(jnp.bfloat16)
    all_tokens, all_cot = (
        lax.all_gather(arm_tokens, "dp", axis=1, tiled=True),
        lax.all_gather(arm_cot, "dp", axis=1, tiled=True),
    )
    group_count = lax.axis_size("dp")
    hidden_width = w_gate.shape[2]
    quarter = hidden_width // group_count
    first_unit = lax.axis_index("dp") * quarter
    gate_share = lax.dynamic_slice_in_dim(w_gate, first_unit, quarter, 2)
    up_share = lax.dynamic_slice_in_dim(w_up, first_unit, quarter, 2)
    down_share = lax.dynamic_slice_in_dim(w_down, first_unit, quarter, 1)
    row_count = arm_tokens.shape[1]
    total_gate = jnp.zeros((local_arms, feature_width, quarter), jnp.float32)
    total_up = jnp.zeros((local_arms, feature_width, quarter), jnp.float32)
    total_down = jnp.zeros((local_arms, quarter, feature_width), jnp.float32)
    for group_index in range(group_count):
        some_tokens = all_tokens[:, group_index * row_count : (group_index + 1) * row_count]
        some_cot = all_cot[:, group_index * row_count : (group_index + 1) * row_count]
        piece_up, piece_act, piece_slope, piece_hidden = arm_forward(
            some_tokens, gate_share, up_share
        )
        piece_dgate, piece_dup = arm_backward(
            piece_up, piece_act, piece_slope, some_cot, down_share
        )
        total_gate = total_gate + rounded(
            jnp.einsum("arc,arh->ach", some_tokens, piece_dgate, preferred_element_type=jnp.float32)
        )
        total_up = total_up + rounded(
            jnp.einsum("arc,arh->ach", some_tokens, piece_dup, preferred_element_type=jnp.float32)
        )
        total_down = total_down + rounded(
            jnp.einsum("arh,arc->ahc", piece_hidden, some_cot, preferred_element_type=jnp.float32)
        )
    grad_gate = total_gate.astype(jnp.bfloat16)
    grad_up = total_up.astype(jnp.bfloat16)
    grad_down = total_down.astype(jnp.bfloat16)
    return (head_output, grad_tokens, grad_gate, grad_up, grad_down)


def mm(left, right):
    return jnp.dot(left, right, preferred_element_type=F32)


def mm_nt(left, right):
    return lax.dot_general(left, right, (((1,), (1,)), ((), ())), preferred_element_type=F32)


def mm_tn(left, right):
    return lax.dot_general(left, right, (((0,), (0,)), ((), ())), preferred_element_type=F32)


def selection(code_tile, arm, capacity):
    count = code_tile.shape[1]
    named = (code_tile == arm).astype(BF16)
    before = lax.broadcasted_iota(jnp.int32, (count, count), 0)
    after = lax.broadcasted_iota(jnp.int32, (count, count), 1)
    ranks = mm(named, (before < after).astype(BF16))
    named = named.astype(F32)
    hit = named[0:1] + named[1:2]
    rank = ranks[0:1] + ranks[1:2]
    slot = lax.broadcasted_iota(jnp.int32, (capacity, count), 0).astype(F32)
    chosen = jnp.where(slot == rank, hit, 0.0)
    share = jnp.sum(
        chosen * (fact_share * named[0:1] + counter_share * named[1:2]), axis=1, keepdims=True
    )
    return chosen.astype(BF16), share


def forward_kernel(blocks, arm_ref, *refs):
    token_refs = refs[:blocks]
    gate_ref, up_ref, down_ref = refs[blocks : blocks + 3]
    keep_ref, give_ref, rows_ref, sel_ref, share_ref, hid_ref, act_ref, slope_ref, total = refs[
        blocks + 3 :
    ]
    step = pl.program_id(0)
    capacity, count = sel_ref.shape[1:]

    @pl.when(step == 0)
    def _():
        arm = arm_ref[0].astype(F32)
        for b in range(blocks):
            chosen, share = selection(
                token_refs[b][count : count + CODE_ROWS, 0:count].astype(F32), arm, capacity
            )
            sel_ref[b] = chosen
            share_ref[b * capacity : (b + 1) * capacity] = jnp.broadcast_to(share, (capacity, 128))
            rows_ref[b * capacity : (b + 1) * capacity] = mm(chosen, token_refs[b][0:count]).astype(
                BF16
            )
        total[...] = jnp.zeros_like(total)

    gate_pre = mm(rows_ref[...], gate_ref[...])
    up_pre = mm(rows_ref[...], up_ref[...])
    sig = jax.nn.sigmoid(gate_pre)
    activated = gate_pre * sig
    hidden = (activated * up_pre).astype(BF16)
    hid_ref[0] = hidden
    act_ref[0] = activated.astype(BF16)
    slope_ref[0] = (up_pre * (sig * (1.0 + gate_pre * (1.0 - sig)))).astype(BF16)
    total[...] += mm(hidden, down_ref[...])

    @pl.when(step == pl.num_programs(0) - 1)
    def _():
        for b in range(blocks):
            at = slice(b * capacity, (b + 1) * capacity)
            out_rows = total[at].astype(BF16).astype(F32) * share_ref[at, 0:1]
            placed = mm_tn(sel_ref[b], out_rows.astype(BF16)).astype(BF16)
            if b < blocks // 2:
                keep_ref[b] = placed
            else:
                give_ref[b - blocks // 2] = placed


def backward_kernel(blocks, *refs):
    cot_refs = refs[:blocks]
    sel_ref, share_ref, act_ref, slope_ref, gate_ref, up_ref, down_ref = refs[blocks : blocks + 7]
    keep_ref, give_ref, cots_ref, dgate_ref, dup_ref, total = refs[blocks + 7 :]
    step = pl.program_id(0)
    capacity, count = sel_ref.shape[1:]

    @pl.when(step == 0)
    def _():
        for b in range(blocks):
            at = slice(b * capacity, (b + 1) * capacity)
            picked = mm(sel_ref[b], cot_refs[b][...])
            cots_ref[at] = (picked * share_ref[at, 0:1]).astype(BF16)
        total[...] = jnp.zeros_like(total)

    d_hidden = mm_nt(cots_ref[...], down_ref[...])
    d_up = (d_hidden * act_ref[0].astype(F32)).astype(BF16)
    d_gate = (d_hidden * slope_ref[0].astype(F32)).astype(BF16)
    dup_ref[0] = d_up
    dgate_ref[0] = d_gate
    total[...] += mm_nt(d_gate, gate_ref[...]) + mm_nt(d_up, up_ref[...])

    @pl.when(step == pl.num_programs(0) - 1)
    def _():
        for b in range(blocks):
            at = slice(b * capacity, (b + 1) * capacity)
            placed = mm_tn(sel_ref[b], total[at].astype(BF16)).astype(BF16)
            if b < blocks // 2:
                keep_ref[b] = placed
            else:
                give_ref[b - blocks // 2] = placed


def weight_kernel(place_ref, rows_ref, cots_ref, hid_ref, dgate_ref, dup_ref, *outs):
    half = rows_ref.shape[1] // 2
    for j, (first, second) in zip((3, 2, 1, 0), zip(outs[0::2], outs[1::2])):
        quarter = place_ref[0] ^ j
        for k, d_ref in enumerate((dgate_ref, dup_ref)):
            part = mm_tn(rows_ref[...], d_ref[quarter]).astype(BF16)
            first[k] = part[:half]
            second[k] = part[half:]
        part = mm_tn(hid_ref[quarter], cots_ref[...]).astype(BF16)
        first[2] = part[:, :half]
        second[2] = part[:, half:]


def vmem():
    return pl.BlockSpec(memory_space=pltpu.VMEM)


def smem():
    return pl.BlockSpec(memory_space=pltpu.SMEM)


def weight_specs(width, chunk):
    tall = pl.BlockSpec((width, chunk), lambda c: (0, c))
    wide = pl.BlockSpec((chunk, width), lambda c: (c, 0))
    return [tall, tall, wide]


def run_forward(arm, tokens, capacity, w_gate, w_up, w_down, chunk):
    blocks = len(tokens)
    width, hidden_width = w_gate.shape
    count = tokens[0].shape[0] - CODE_ROWS
    rows = blocks * capacity
    steps = hidden_width // chunk
    whole = lambda *shape: pl.BlockSpec(shape, lambda c: (0,) * len(shape))
    piece = pl.BlockSpec((1, rows, chunk), lambda c: (c, 0, 0))
    return pl.pallas_call(
        functools.partial(forward_kernel, blocks),
        grid=(steps,),
        in_specs=[smem()]
        + [whole(*tokens[0].shape)] * blocks
        + weight_specs(width, chunk),
        out_specs=[whole(blocks // 2, count, width)] * 2
        + [whole(rows, width), whole(blocks, capacity, count), whole(rows, 128)]
        + [piece] * 3,
        out_shape=[jax.ShapeDtypeStruct((blocks // 2, count, width), BF16)] * 2
        + [
            jax.ShapeDtypeStruct((rows, width), BF16),
            jax.ShapeDtypeStruct((blocks, capacity, count), BF16),
            jax.ShapeDtypeStruct((rows, 128), F32),
        ]
        + [jax.ShapeDtypeStruct((steps, rows, chunk), BF16)] * 3,
        scratch_shapes=[pltpu.VMEM((rows, width), F32)],
        compiler_params=pltpu.CompilerParams(vmem_limit_bytes=VMEM_BYTES),
        cost_estimate=pl.CostEstimate(
            flops=6 * rows * width * hidden_width, bytes_accessed=8 << 20, transcendentals=0
        ),
        name="arm_forward",
    )(arm, *tokens, w_gate, w_up, w_down)


def run_backward(cots, sel, share, act, slope, w_gate, w_up, w_down, chunk):
    blocks = len(cots)
    width, hidden_width = w_gate.shape
    capacity, count = sel.shape[1:]
    rows = blocks * capacity
    steps = hidden_width // chunk
    whole = lambda *shape: pl.BlockSpec(shape, lambda c: (0,) * len(shape))
    piece = pl.BlockSpec((1, rows, chunk), lambda c: (c, 0, 0))
    return pl.pallas_call(
        functools.partial(backward_kernel, blocks),
        grid=(steps,),
        in_specs=[whole(count, width)] * blocks
        + [whole(*sel.shape), whole(*share.shape), piece, piece]
        + weight_specs(width, chunk),
        out_specs=[whole(blocks // 2, count, width)] * 2 + [whole(rows, width), piece, piece],
        out_shape=[jax.ShapeDtypeStruct((blocks // 2, count, width), BF16)] * 2
        + [jax.ShapeDtypeStruct((rows, width), BF16)]
        + [jax.ShapeDtypeStruct((steps, rows, chunk), BF16)] * 2,
        scratch_shapes=[pltpu.VMEM((rows, width), F32)],
        compiler_params=pltpu.CompilerParams(vmem_limit_bytes=VMEM_BYTES),
        cost_estimate=pl.CostEstimate(
            flops=6 * rows * width * hidden_width, bytes_accessed=8 << 20, transcendentals=0
        ),
        name="arm_backward",
    )(*cots, sel, share, act, slope, w_gate, w_up, w_down)


def run_weights(place, rows, cots, hid, dgate, dup):
    width = rows.shape[1]
    chunk = hid.shape[2]
    return pl.pallas_call(
        weight_kernel,
        in_specs=[smem()] + [vmem()] * 5,
        out_specs=[vmem()] * 8,
        out_shape=[jax.ShapeDtypeStruct((3, width // 2, chunk), BF16)] * 8,
        compiler_params=pltpu.CompilerParams(vmem_limit_bytes=VMEM_BYTES),
        cost_estimate=pl.CostEstimate(
            flops=6 * rows.shape[0] * width * hid.shape[0] * chunk,
            bytes_accessed=8 << 20,
            transcendentals=0,
        ),
        name="arm_weights",
    )(place, rows, cots, hid, dgate, dup)


def on_line(tokens, codes, cotangent, w_gate, w_up, w_down):
    token_count, width = tokens.shape
    arm_count = lax.axis_size("expert")
    capacity = 4 * token_count // arm_count
    w_gate, w_up, w_down = w_gate[0], w_up[0], w_down[0]
    hidden_width = w_gate.shape[1]
    chunk = hidden_width // lax.axis_size("dp")
    expert = lax.axis_index("expert")
    arm = jnp.reshape(expert, (1,)).astype(jnp.int32)
    place = jnp.reshape(lax.axis_index("dp"), (1,)).astype(jnp.int32)
    z = expert // 2
    edge = (z == 0) | (z == 3)

    def along(pairs):
        return [(2 * s + c, 2 * d + c) for s, d in pairs for c in (0, 1)]

    far = along([(0, 3), (3, 0), (1, 2), (2, 1)])
    near = along([(0, 1), (1, 0), (2, 3), (3, 2)])
    skip = along([(0, 2), (2, 3), (3, 1), (1, 0)])
    skip_back = along([(2, 0), (3, 2), (1, 3), (0, 1)])
    core = [(e, e ^ 1) for e in range(8)]
    x_pair = [(i, i ^ 1) for i in range(4)]
    y_pair = [(i, i ^ 2) for i in range(4)]
    send = lambda value, pairs: lax.ppermute(value, "expert", pairs)
    send_dp = lambda value, pairs: lax.ppermute(value, "dp", pairs)

    code_rows = jnp.pad(
        codes.T.astype(BF16), ((0, CODE_ROWS - 2), (0, width - token_count))
    )
    token_part = jnp.concatenate([tokens, code_rows], axis=0)

    def gather(own):
        from_far = send(own, far)
        from_near = send(own, near)
        from_skip = send(jnp.where(edge, own, from_far), skip)
        mine = [own, from_far, from_near, from_skip]
        return mine + [send(part, core) for part in mine]

    all_tokens = gather(token_part)
    all_cots = gather(cotangent)

    head_keep, head_give, rows, sel, share, hid, act, slope = run_forward(
        arm, all_tokens, capacity, w_gate, w_up, w_down, chunk
    )
    grad_keep, grad_give, cots, dgate, dup = run_backward(
        all_cots, sel, share, act, slope, w_gate, w_up, w_down, chunk
    )

    def reduce(keep, give):
        got = send(give, core)
        both = [keep[k].astype(F32) + got[k].astype(F32) for k in range(4)]
        own, for_far, for_near, for_skip = both
        from_skip = send(for_skip.astype(BF16), skip_back).astype(F32)
        from_near = send(for_near.astype(BF16), near).astype(F32)
        for_far = for_far + jnp.where(edge, 0.0, from_skip)
        from_far = send(for_far.astype(BF16), far).astype(F32)
        return (own + from_near + from_far + jnp.where(edge, from_skip, 0.0)).astype(BF16)

    head_output = reduce(head_keep, head_give)
    grad_tokens = reduce(grad_keep, grad_give)

    d0, d1, y0, y1, x0, x1, k0, k1 = run_weights(place, rows, cots, hid, dgate, dup)
    add = lambda a, b: a.astype(F32) + b.astype(F32)
    y0 = add(y0, send_dp(d0, x_pair))
    x1 = add(x1, send_dp(d1, y_pair))
    k0 = add(k0, send_dp(x0, x_pair))
    k1 = add(k1, send_dp(y1, y_pair))
    k0 = add(k0, send_dp(y0.astype(BF16), y_pair)).astype(BF16)
    k1 = add(k1, send_dp(x1.astype(BF16), x_pair)).astype(BF16)
    grad_gate = jnp.concatenate([k0[0], k1[0]], axis=0)[None]
    grad_up = jnp.concatenate([k0[1], k1[1]], axis=0)[None]
    grad_down = jnp.concatenate([k0[2], k1[2]], axis=1)[None]
    return (head_output, grad_tokens, grad_gate, grad_up, grad_down)


def solution(mesh):
    on_square_of_lines = mesh.shape["dp"] == 4 and mesh.shape["expert"] == 8
    return jax.shard_map(
        on_line if on_square_of_lines else on_device,
        mesh=mesh,
        in_specs=(
            P(("dp", "expert"), None),
            P(("dp", "expert"), None),
            P(("dp", "expert"), None),
            P("expert", None, None),
            P("expert", None, None),
            P("expert", None, None),
        ),
        out_specs=(
            P(("dp", "expert"), None),
            P(("dp", "expert"), None),
            P("expert", None, "dp"),
            P("expert", None, "dp"),
            P("expert", "dp", None),
        ),
        check_vma=False,
    )
```

```python
import functools

import jax
import jax.numpy as jnp
from jax import lax
from jax.experimental import pallas as pl
from jax.experimental.pallas import tpu as pltpu
from jax.sharding import PartitionSpec as P

fact_share = 0.7
counter_share = 0.3

F32 = jnp.float32
BF16 = jnp.bfloat16
CODE_ROWS = 16
VMEM_BYTES = 56 * 1024 * 1024

def rounded(value):
    return lax.optimization_barrier(value.astype(jnp.bfloat16)).astype(jnp.float32)


def silu_parts(gate_pre):
    sigmoid_gate = jax.nn.sigmoid(gate_pre)
    return (gate_pre * sigmoid_gate, sigmoid_gate * (1.0 + gate_pre * (1.0 - sigmoid_gate)))


def arm_forward(rows_in, gate_w, up_w):
    gate_pre = jnp.einsum("arc,ach->arh", rows_in, gate_w, preferred_element_type=jnp.float32)
    up_pre = jnp.einsum("arc,ach->arh", rows_in, up_w, preferred_element_type=jnp.float32)
    activated, silu_slope = silu_parts(gate_pre)
    hidden = (activated * up_pre).astype(jnp.bfloat16)
    return (up_pre, activated, silu_slope, hidden)


def arm_backward(up_pre, activated, silu_slope, cot_in, down_w):
    d_hidden = jnp.einsum("arc,ahc->arh", cot_in, down_w, preferred_element_type=jnp.float32)
    d_up = (d_hidden * activated).astype(jnp.bfloat16)
    d_gate = (d_hidden * up_pre * silu_slope).astype(jnp.bfloat16)
    return (d_gate, d_up)


def on_device(tokens, codes, cotangent, w_gate, w_up, w_down):
    token_count, feature_width = tokens.shape
    local_arms = w_gate.shape[0]
    arm_count = local_arms * lax.axis_size("expert")
    capacity = 4 * token_count // arm_count
    flat_codes = codes.reshape(-1)
    arm_ids = jnp.arange(arm_count, dtype=jnp.int32)
    onehot = (flat_codes[:, None] == arm_ids[None, :]).astype(jnp.int32)
    earlier = jnp.cumsum(onehot, axis=0) - onehot
    destination = flat_codes * capacity + jnp.sum(earlier * onehot, axis=1)
    shares = jnp.tile(jnp.array([fact_share, counter_share], jnp.float32), token_count)
    token_rows = jnp.repeat(tokens, 2, axis=0)
    cot_rows = (jnp.repeat(cotangent.astype(jnp.float32), 2, axis=0) * shares[:, None]).astype(
        jnp.bfloat16
    )
    blank_rows = jnp.zeros((arm_count * capacity, feature_width), jnp.bfloat16)
    send_tokens = (
        blank_rows.at[destination].set(token_rows).reshape(arm_count, capacity, feature_width)
    )
    send_cot = blank_rows.at[destination].set(cot_rows).reshape(arm_count, capacity, feature_width)
    arm_tokens, arm_cot = (
        lax.all_to_all(send_tokens, "expert", split_axis=0, concat_axis=1, tiled=True),
        lax.all_to_all(send_cot, "expert", split_axis=0, concat_axis=1, tiled=True),
    )
    up_pre, activated, silu_slope, hidden = arm_forward(arm_tokens, w_gate, w_up)
    out_rows = jnp.einsum(
        "arh,ahc->arc", hidden, w_down, preferred_element_type=jnp.float32
    ).astype(jnp.bfloat16)
    d_gate, d_up = arm_backward(up_pre, activated, silu_slope, arm_cot, w_down)
    input_rows = (
        jnp.einsum("arh,ach->arc", d_gate, w_gate, preferred_element_type=jnp.float32)
        + jnp.einsum("arh,ach->arc", d_up, w_up, preferred_element_type=jnp.float32)
    ).astype(jnp.bfloat16)
    back_out, back_input = (
        lax.all_to_all(out_rows, "expert", split_axis=1, concat_axis=0, tiled=True),
        lax.all_to_all(input_rows, "expert", split_axis=1, concat_axis=0, tiled=True),
    )
    back_out = back_out.reshape(arm_count * capacity, feature_width)[destination]
    back_out = back_out.reshape(token_count, 2, feature_width).astype(jnp.float32)
    back_input = back_input.reshape(arm_count * capacity, feature_width)[destination]
    back_input = back_input.reshape(token_count, 2, feature_width).astype(jnp.float32)
    head_output = (fact_share * back_out[:, 0] + counter_share * back_out[:, 1]).astype(
        jnp.bfloat16
    )
    grad_tokens = (back_input[:, 0] + back_input[:, 1]).astype(jnp.bfloat16)
    all_tokens, all_cot = (
        lax.all_gather(arm_tokens, "dp", axis=1, tiled=True),
        lax.all_gather(arm_cot, "dp", axis=1, tiled=True),
    )
    group_count = lax.axis_size("dp")
    hidden_width = w_gate.shape[2]
    quarter = hidden_width // group_count
    first_unit = lax.axis_index("dp") * quarter
    gate_share = lax.dynamic_slice_in_dim(w_gate, first_unit, quarter, 2)
    up_share = lax.dynamic_slice_in_dim(w_up, first_unit, quarter, 2)
    down_share = lax.dynamic_slice_in_dim(w_down, first_unit, quarter, 1)
    row_count = arm_tokens.shape[1]
    total_gate = jnp.zeros((local_arms, feature_width, quarter), jnp.float32)
    total_up = jnp.zeros((local_arms, feature_width, quarter), jnp.float32)
    total_down = jnp.zeros((local_arms, quarter, feature_width), jnp.float32)
    for group_index in range(group_count):
        some_tokens = all_tokens[:, group_index * row_count : (group_index + 1) * row_count]
        some_cot = all_cot[:, group_index * row_count : (group_index + 1) * row_count]
        piece_up, piece_act, piece_slope, piece_hidden = arm_forward(
            some_tokens, gate_share, up_share
        )
        piece_dgate, piece_dup = arm_backward(
            piece_up, piece_act, piece_slope, some_cot, down_share
        )
        total_gate = total_gate + rounded(
            jnp.einsum("arc,arh->ach", some_tokens, piece_dgate, preferred_element_type=jnp.float32)
        )
        total_up = total_up + rounded(
            jnp.einsum("arc,arh->ach", some_tokens, piece_dup, preferred_element_type=jnp.float32)
        )
        total_down = total_down + rounded(
            jnp.einsum("arh,arc->ahc", piece_hidden, some_cot, preferred_element_type=jnp.float32)
        )
    grad_gate = total_gate.astype(jnp.bfloat16)
    grad_up = total_up.astype(jnp.bfloat16)
    grad_down = total_down.astype(jnp.bfloat16)
    return (head_output, grad_tokens, grad_gate, grad_up, grad_down)


def mm(left, right):
    return jnp.dot(left, right, preferred_element_type=F32)


def mm_nt(left, right):
    return lax.dot_general(left, right, (((1,), (1,)), ((), ())), preferred_element_type=F32)


def mm_tn(left, right):
    return lax.dot_general(left, right, (((0,), (0,)), ((), ())), preferred_element_type=F32)


def selections(code_tiles, arm, capacity):
    count = code_tiles[0].shape[1]
    named = [(tile.astype(F32) == arm).astype(F32) for tile in code_tiles]
    before = lax.broadcasted_iota(jnp.int32, (count, count), 0)
    after = lax.broadcasted_iota(jnp.int32, (count, count), 1)
    ranks = mm(jnp.concatenate(named, axis=0).astype(BF16), (before < after).astype(BF16))
    slot = lax.broadcasted_iota(jnp.int32, (capacity, count), 0).astype(F32)
    pairs = []
    for b, hit in enumerate(named):
        rank = ranks[b * CODE_ROWS : b * CODE_ROWS + 1] + ranks[b * CODE_ROWS + 1 : b * CODE_ROWS + 2]
        here = slot == rank
        pairs.append((jnp.where(here, hit[0:1], 0.0), jnp.where(here, hit[1:2], 0.0)))
    return pairs


def pack_kernel(tokens_ref, cot_ref, codes_ref, out_ref):
    count = tokens_ref.shape[0]
    out_ref[0:count] = tokens_ref[...]
    out_ref[count : 2 * count] = cot_ref[...]
    out_ref[2 * count : 2 * count + CODE_ROWS] = jnp.zeros((CODE_ROWS, out_ref.shape[1]), BF16)
    rows = lax.broadcasted_iota(jnp.int32, (CODE_ROWS, count), 0)
    codes = codes_ref[...].astype(F32)
    both = jnp.where(rows == 0, codes[0:1], jnp.where(rows == 1, codes[1:2], 0.0))
    out_ref[2 * count : 2 * count + CODE_ROWS, 0:count] = both.astype(BF16)


def arm_kernel(blocks, ins, outs_count, scalar_ref, *refs):
    sources, refs = refs[:ins], refs[ins:]
    outs, refs = refs[:outs_count], refs[outs_count:]
    in_sems, out_sems, sel = refs[-3:]
    staged, refs = refs[-3 - outs_count : -3], refs[: -3 - outs_count]
    held, (gate_ref, up_ref, down_ref), saved = refs[0], refs[1:4], refs[4:]
    keep_ref, give_ref = staged[:2]
    rows, cots, hid, dgate, dup = saved[5:] if saved else staged[2:]
    capacity, count = sel.shape[1], sel.shape[2] // 2
    pieces = hid.shape[0]
    targets = [held.at[b] for b in range(blocks)] + [gate_ref, up_ref, down_ref, *saved[:5]]
    loads = [
        pltpu.make_async_copy(source, target, in_sems.at[k])
        for k, (source, target) in enumerate(zip(sources, targets))
    ]
    stores = [
        pltpu.make_async_copy(source, target, out_sems.at[k])
        for k, (source, target) in enumerate(zip(staged, outs))
    ]
    for load in loads:
        load.start()
    for load in loads[:blocks]:
        load.wait()

    tiles = [held[b, 2 * count : 2 * count + CODE_ROWS, 0:count] for b in range(blocks)]
    pairs = selections(tiles, scalar_ref[0].astype(F32), capacity)
    for b, (fact, counter) in enumerate(pairs):
        at = slice(b * capacity, (b + 1) * capacity)
        sel[b] = jnp.concatenate([fact, counter], axis=1).astype(BF16)
        rows[at] = mm((fact + counter).astype(BF16), held[b, 0:count]).astype(BF16)
        cot = held[b, count : 2 * count].astype(F32)
        scaled = jnp.concatenate(
            [(fact_share * cot).astype(BF16), (counter_share * cot).astype(BF16)], axis=0
        )
        cots[at] = mm(sel[b], scaled).astype(BF16)

    for load in loads[blocks : blocks + 3]:
        load.wait()
    for k in range(pieces):
        piece = hid.shape[2]
        cut = slice(k * piece, (k + 1) * piece)
        gate_pre = mm(rows[...], gate_ref[:, cut])
        up_pre = mm(rows[...], up_ref[:, cut])
        d_hidden = mm_nt(cots[...], down_ref[cut, :])
        sig = 0.5 * jnp.tanh(0.5 * gate_pre) + 0.5
        activated = gate_pre * sig
        hid[k] = (activated * up_pre).astype(BF16)
        dup[k] = (d_hidden * activated).astype(BF16)
        dgate[k] = (d_hidden * up_pre * (sig + activated * (1.0 - sig))).astype(BF16)
    if not saved:
        for store in stores[2:]:
            store.start()

    total_out, total_in = None, None
    for k in range(pieces):
        cut = slice(k * piece, (k + 1) * piece)
        out_part = mm(hid[k], down_ref[cut, :])
        in_part = mm_nt(dgate[k], gate_ref[:, cut]) + mm_nt(dup[k], up_ref[:, cut])
        total_out = out_part if k == 0 else total_out + out_part
        total_in = in_part if k == 0 else total_in + in_part
    for b in range(blocks):
        at = slice(b * capacity, (b + 1) * capacity)
        target = keep_ref if b < blocks // 2 else give_ref
        placed = mm_tn(sel[b], total_out[at].astype(BF16))
        target[b % (blocks // 2), 0] = (
            fact_share * placed[:count] + counter_share * placed[count:]
        ).astype(BF16)
        placed = mm_tn(sel[b], total_in[at].astype(BF16))
        target[b % (blocks // 2), 1] = (placed[:count] + placed[count:]).astype(BF16)
    stores[0].start()
    stores[1].start()

    if saved:
        for load in loads[blocks + 3 :]:
            load.wait()
        x_ref, y_ref, x_next_ref, y_next_ref, first_ref, second_ref = staged[2:]
        all_rows = jnp.concatenate([saved[0][...], rows[...]], axis=0)
        all_cots = jnp.concatenate([saved[1][...], cots[...]], axis=0)
        half = all_rows.shape[1] // 2
        quarters = (
            (3, x_ref.at[0], y_ref.at[0], ()),
            (1, x_ref.at[1], x_next_ref, (2, 4)),
            (2, y_next_ref, y_ref.at[1], (5, 3)),
            (0, first_ref, second_ref, (6, 7)),
        )
        for j, first, second, complete in quarters:
            quarter = scalar_ref[1] ^ j
            both = lambda old, new: jnp.concatenate([old[quarter], new[quarter]], axis=0)
            for k, d_pre in enumerate((both(saved[3], dgate), both(saved[4], dup))):
                part = mm_tn(all_rows, d_pre).astype(BF16)
                first[k] = part[:half]
                second[k] = part[half:]
            part = mm_tn(both(saved[2], hid), all_cots).astype(BF16)
            first[2] = part[:, :half]
            second[2] = part[:, half:]
            for k in complete:
                stores[k].start()
    for store in stores:
        store.wait()


def vmem():
    return pl.BlockSpec(memory_space=pltpu.VMEM)


def smem():
    return pl.BlockSpec(memory_space=pltpu.SMEM)


def run_pack(tokens, cotangent, codes):
    count, width = tokens.shape
    return pl.pallas_call(
        pack_kernel,
        in_specs=[vmem()] * 3,
        out_specs=vmem(),
        out_shape=jax.ShapeDtypeStruct((2 * count + CODE_ROWS, width), BF16),
        name="pack",
    )(tokens, cotangent, codes.T)


def run_arm(scalars, parts, capacity, weights, piece, saved=()):
    blocks = len(parts)
    width, hidden_width = weights[0].shape
    count = (parts[0].shape[0] - CODE_ROWS) // 2
    rows = blocks * capacity
    pieces = hidden_width // piece
    one = (3, width // 2, piece)
    made = [(rows, width)] * 2 + [(pieces, rows, piece)] * 3
    outs = [(blocks // 2, 2, count, width)] * 2
    outs += [(2,) + one] * 2 + [one] * 4 if saved else made
    held = [(blocks,) + parts[0].shape] + [weight.shape for weight in weights]
    held += [array.shape for array in saved] + made if saved else []
    sources = (*parts, *weights, *saved)
    anywhere = pl.BlockSpec(memory_space=pl.ANY)
    return pl.pallas_call(
        functools.partial(arm_kernel, blocks, len(sources), len(outs)),
        in_specs=[smem()] + [anywhere] * len(sources),
        out_specs=[anywhere] * len(outs),
        out_shape=[jax.ShapeDtypeStruct(shape, BF16) for shape in outs],
        scratch_shapes=[pltpu.VMEM(shape, BF16) for shape in held + outs]
        + [
            pltpu.SemaphoreType.DMA((len(sources),)),
            pltpu.SemaphoreType.DMA((len(outs),)),
            pltpu.VMEM((blocks, capacity, 2 * count), BF16),
        ],
        compiler_params=pltpu.CompilerParams(vmem_limit_bytes=VMEM_BYTES),
        cost_estimate=pl.CostEstimate(
            flops=(24 if saved else 12) * rows * width * hidden_width,
            bytes_accessed=12 << 20,
            transcendentals=0,
        ),
        name="arm_late" if saved else "arm_early",
    )(scalars, *sources)


def on_line(tokens, codes, cotangent, w_gate, w_up, w_down):
    token_count, width = tokens.shape
    arm_count = lax.axis_size("expert")
    capacity = 4 * token_count // arm_count
    w_gate, w_up, w_down = w_gate[0], w_up[0], w_down[0]
    hidden_width = w_gate.shape[1]
    chunk = hidden_width // lax.axis_size("dp")
    expert = lax.axis_index("expert")
    arm = jnp.reshape(expert, (1,)).astype(jnp.int32)
    place = jnp.reshape(lax.axis_index("dp"), (1,)).astype(jnp.int32)
    z = expert // 2
    edge = (z == 0) | (z == 3)

    def along(pairs):
        return [(2 * s + c, 2 * d + c) for s, d in pairs for c in (0, 1)]

    far = along([(0, 3), (3, 0), (1, 2), (2, 1)])
    near = along([(0, 1), (1, 0), (2, 3), (3, 2)])
    skip = along([(0, 2), (2, 3), (3, 1), (1, 0)])
    skip_back = along([(2, 0), (3, 2), (1, 3), (0, 1)])
    core = [(e, e ^ 1) for e in range(8)]
    x_pair = [(i, i ^ 1) for i in range(4)]
    y_pair = [(i, i ^ 2) for i in range(4)]
    send = lambda value, pairs: lax.ppermute(value, "expert", pairs)
    send_dp = lambda value, pairs: lax.ppermute(value, "dp", pairs)

    own = run_pack(tokens, cotangent, codes)
    add = lambda a, b: a.astype(F32) + b.astype(F32)
    run = functools.partial(
        run_arm,
        jnp.concatenate([arm, place]),
        capacity=capacity,
        weights=(w_gate, w_up, w_down),
        piece=chunk,
    )
    from_far = send(own, far)
    from_near = send(own, near)
    keep, give, *saved = run([own, from_near, send(own, core), send(from_near, core)])
    from_skip = send(jnp.where(edge, own, from_far), skip)
    from_skip, keep = lax.optimization_barrier((from_skip, keep))
    got = send(give, core)
    for_own = add(keep[0], got[0])
    for_near = add(keep[1], got[1]).astype(BF16)
    keep, give, x_part, y_part, x_next, y_next, k0, k1 = run(
        [from_far, from_skip, send(from_far, core), send(from_skip, core)], saved=saved
    )
    got = send(give, core)
    for_far = add(keep[0], got[0])
    for_skip = add(keep[1], got[1]).astype(BF16)
    from_x = send_dp(x_part, x_pair)
    from_y = send_dp(y_part, y_pair)
    from_skip = send(for_skip, skip_back).astype(F32)
    from_near = send(for_near, near)
    for_far = for_far + jnp.where(edge, 0.0, from_skip)
    from_far = send(for_far.astype(BF16), far)
    result = for_own + from_near + from_far + jnp.where(edge, from_skip, 0.0)
    head_output, grad_tokens = result[0].astype(BF16), result[1].astype(BF16)
    y_next = add(y_next, from_x[0]).astype(BF16)
    x_next = add(x_next, from_y[0]).astype(BF16)
    k0 = (add(k0, from_x[1]) + send_dp(y_next, y_pair)).astype(BF16)
    k1 = (add(k1, from_y[1]) + send_dp(x_next, x_pair)).astype(BF16)
    grad_gate = jnp.concatenate([k0[0], k1[0]], axis=0)[None]
    grad_up = jnp.concatenate([k0[1], k1[1]], axis=0)[None]
    grad_down = jnp.concatenate([k0[2], k1[2]], axis=1)[None]
    return (head_output, grad_tokens, grad_gate, grad_up, grad_down)


def solution(mesh):
    on_square_of_lines = mesh.shape["dp"] == 4 and mesh.shape["expert"] == 8
    return jax.shard_map(
        on_line if on_square_of_lines else on_device,
        mesh=mesh,
        in_specs=(
            P(("dp", "expert"), None),
            P(("dp", "expert"), None),
            P(("dp", "expert"), None),
            P("expert", None, None),
            P("expert", None, None),
            P("expert", None, None),
        ),
        out_specs=(
            P(("dp", "expert"), None),
            P(("dp", "expert"), None),
            P("expert", None, "dp"),
            P("expert", None, "dp"),
            P("expert", "dp", None),
        ),
        check_vma=False,
    )
```

```python
import functools

import jax
import jax.numpy as jnp
from jax import lax
from jax.experimental import pallas as pl
from jax.experimental.pallas import tpu as pltpu
from jax.sharding import PartitionSpec as P

fact_share = 0.7
counter_share = 0.3

F32 = jnp.float32
BF16 = jnp.bfloat16
CODE_ROWS = 16
VMEM_BYTES = 56 * 1024 * 1024

def rounded(value):
    return lax.optimization_barrier(value.astype(jnp.bfloat16)).astype(jnp.float32)


def silu_parts(gate_pre):
    sigmoid_gate = jax.nn.sigmoid(gate_pre)
    return (gate_pre * sigmoid_gate, sigmoid_gate * (1.0 + gate_pre * (1.0 - sigmoid_gate)))


def arm_forward(rows_in, gate_w, up_w):
    gate_pre = jnp.einsum("arc,ach->arh", rows_in, gate_w, preferred_element_type=jnp.float32)
    up_pre = jnp.einsum("arc,ach->arh", rows_in, up_w, preferred_element_type=jnp.float32)
    activated, silu_slope = silu_parts(gate_pre)
    hidden = (activated * up_pre).astype(jnp.bfloat16)
    return (up_pre, activated, silu_slope, hidden)


def arm_backward(up_pre, activated, silu_slope, cot_in, down_w):
    d_hidden = jnp.einsum("arc,ahc->arh", cot_in, down_w, preferred_element_type=jnp.float32)
    d_up = (d_hidden * activated).astype(jnp.bfloat16)
    d_gate = (d_hidden * up_pre * silu_slope).astype(jnp.bfloat16)
    return (d_gate, d_up)


def on_device(tokens, codes, cotangent, w_gate, w_up, w_down):
    token_count, feature_width = tokens.shape
    local_arms = w_gate.shape[0]
    arm_count = local_arms * lax.axis_size("expert")
    capacity = 4 * token_count // arm_count
    flat_codes = codes.reshape(-1)
    arm_ids = jnp.arange(arm_count, dtype=jnp.int32)
    onehot = (flat_codes[:, None] == arm_ids[None, :]).astype(jnp.int32)
    earlier = jnp.cumsum(onehot, axis=0) - onehot
    destination = flat_codes * capacity + jnp.sum(earlier * onehot, axis=1)
    shares = jnp.tile(jnp.array([fact_share, counter_share], jnp.float32), token_count)
    token_rows = jnp.repeat(tokens, 2, axis=0)
    cot_rows = (jnp.repeat(cotangent.astype(jnp.float32), 2, axis=0) * shares[:, None]).astype(
        jnp.bfloat16
    )
    blank_rows = jnp.zeros((arm_count * capacity, feature_width), jnp.bfloat16)
    send_tokens = (
        blank_rows.at[destination].set(token_rows).reshape(arm_count, capacity, feature_width)
    )
    send_cot = blank_rows.at[destination].set(cot_rows).reshape(arm_count, capacity, feature_width)
    arm_tokens, arm_cot = (
        lax.all_to_all(send_tokens, "expert", split_axis=0, concat_axis=1, tiled=True),
        lax.all_to_all(send_cot, "expert", split_axis=0, concat_axis=1, tiled=True),
    )
    up_pre, activated, silu_slope, hidden = arm_forward(arm_tokens, w_gate, w_up)
    out_rows = jnp.einsum(
        "arh,ahc->arc", hidden, w_down, preferred_element_type=jnp.float32
    ).astype(jnp.bfloat16)
    d_gate, d_up = arm_backward(up_pre, activated, silu_slope, arm_cot, w_down)
    input_rows = (
        jnp.einsum("arh,ach->arc", d_gate, w_gate, preferred_element_type=jnp.float32)
        + jnp.einsum("arh,ach->arc", d_up, w_up, preferred_element_type=jnp.float32)
    ).astype(jnp.bfloat16)
    back_out, back_input = (
        lax.all_to_all(out_rows, "expert", split_axis=1, concat_axis=0, tiled=True),
        lax.all_to_all(input_rows, "expert", split_axis=1, concat_axis=0, tiled=True),
    )
    back_out = back_out.reshape(arm_count * capacity, feature_width)[destination]
    back_out = back_out.reshape(token_count, 2, feature_width).astype(jnp.float32)
    back_input = back_input.reshape(arm_count * capacity, feature_width)[destination]
    back_input = back_input.reshape(token_count, 2, feature_width).astype(jnp.float32)
    head_output = (fact_share * back_out[:, 0] + counter_share * back_out[:, 1]).astype(
        jnp.bfloat16
    )
    grad_tokens = (back_input[:, 0] + back_input[:, 1]).astype(jnp.bfloat16)
    all_tokens, all_cot = (
        lax.all_gather(arm_tokens, "dp", axis=1, tiled=True),
        lax.all_gather(arm_cot, "dp", axis=1, tiled=True),
    )
    group_count = lax.axis_size("dp")
    hidden_width = w_gate.shape[2]
    quarter = hidden_width // group_count
    first_unit = lax.axis_index("dp") * quarter
    gate_share = lax.dynamic_slice_in_dim(w_gate, first_unit, quarter, 2)
    up_share = lax.dynamic_slice_in_dim(w_up, first_unit, quarter, 2)
    down_share = lax.dynamic_slice_in_dim(w_down, first_unit, quarter, 1)
    row_count = arm_tokens.shape[1]
    total_gate = jnp.zeros((local_arms, feature_width, quarter), jnp.float32)
    total_up = jnp.zeros((local_arms, feature_width, quarter), jnp.float32)
    total_down = jnp.zeros((local_arms, quarter, feature_width), jnp.float32)
    for group_index in range(group_count):
        some_tokens = all_tokens[:, group_index * row_count : (group_index + 1) * row_count]
        some_cot = all_cot[:, group_index * row_count : (group_index + 1) * row_count]
        piece_up, piece_act, piece_slope, piece_hidden = arm_forward(
            some_tokens, gate_share, up_share
        )
        piece_dgate, piece_dup = arm_backward(
            piece_up, piece_act, piece_slope, some_cot, down_share
        )
        total_gate = total_gate + rounded(
            jnp.einsum("arc,arh->ach", some_tokens, piece_dgate, preferred_element_type=jnp.float32)
        )
        total_up = total_up + rounded(
            jnp.einsum("arc,arh->ach", some_tokens, piece_dup, preferred_element_type=jnp.float32)
        )
        total_down = total_down + rounded(
            jnp.einsum("arh,arc->ahc", piece_hidden, some_cot, preferred_element_type=jnp.float32)
        )
    grad_gate = total_gate.astype(jnp.bfloat16)
    grad_up = total_up.astype(jnp.bfloat16)
    grad_down = total_down.astype(jnp.bfloat16)
    return (head_output, grad_tokens, grad_gate, grad_up, grad_down)


def mm(left, right):
    return jnp.dot(left, right, preferred_element_type=F32)


def mm_nt(left, right):
    return lax.dot_general(left, right, (((1,), (1,)), ((), ())), preferred_element_type=F32)


def mm_tn(left, right):
    return lax.dot_general(left, right, (((0,), (0,)), ((), ())), preferred_element_type=F32)


def selections(code_tiles, arm, capacity):
    count = code_tiles[0].shape[1]
    named = [(tile.astype(F32) == arm).astype(F32) for tile in code_tiles]
    before = lax.broadcasted_iota(jnp.int32, (count, count), 0)
    after = lax.broadcasted_iota(jnp.int32, (count, count), 1)
    ranks = mm(jnp.concatenate(named, axis=0).astype(BF16), (before < after).astype(BF16))
    slot = lax.broadcasted_iota(jnp.int32, (capacity, count), 0).astype(F32)
    chosen, shares = [], []
    for b, hit in enumerate(named):
        rank = ranks[b * CODE_ROWS : b * CODE_ROWS + 1] + ranks[b * CODE_ROWS + 1 : b * CODE_ROWS + 2]
        here = jnp.where(slot == rank, hit[0:1] + hit[1:2], 0.0)
        share = fact_share * hit[0:1] + counter_share * hit[1:2]
        chosen.append(here.astype(BF16))
        shares.append(jnp.sum(here * share, axis=1, keepdims=True))
    return chosen, shares


def pack_kernel(tokens_ref, cot_ref, codes_ref, out_ref):
    count = tokens_ref.shape[0]
    out_ref[0:count] = tokens_ref[...]
    out_ref[count : 2 * count] = cot_ref[...]
    out_ref[2 * count : 2 * count + CODE_ROWS] = jnp.zeros((CODE_ROWS, out_ref.shape[1]), BF16)
    rows = lax.broadcasted_iota(jnp.int32, (CODE_ROWS, count), 0)
    codes = codes_ref[...].astype(F32)
    both = jnp.where(rows == 0, codes[0:1], jnp.where(rows == 1, codes[1:2], 0.0))
    out_ref[2 * count : 2 * count + CODE_ROWS, 0:count] = both.astype(BF16)


def arm_kernel(blocks, ins, outs_count, *refs):
    sources, refs = refs[:ins], refs[ins:]
    outs, refs = refs[:outs_count], refs[outs_count:]
    in_sems, out_sems = refs[-2:]
    staged, refs = refs[-2 - outs_count : -2], refs[: -2 - outs_count]
    held, (gate_ref, up_ref, down_ref), saved = refs[0], refs[1:4], refs[4:]
    keep_ref, give_ref = staged[:2]
    rows, cots, hid, dgate, dup = saved[5:] if saved else staged[2:]
    capacity, count = rows.shape[0] // blocks, keep_ref.shape[2]
    pieces = hid.shape[0]
    targets = [held.at[b] for b in range(blocks)] + [gate_ref, up_ref, down_ref, *saved[:5]]
    loads = [
        pltpu.make_async_copy(source, target, in_sems.at[k])
        for k, (source, target) in enumerate(zip(sources, targets))
    ]
    stores = [
        pltpu.make_async_copy(source, target, out_sems.at[k])
        for k, (source, target) in enumerate(zip(staged, outs))
    ]
    for load in loads:
        load.start()
    arm, place = lax.axis_index("expert"), lax.axis_index("dp")
    for load in loads[:blocks]:
        load.wait()

    tiles = [held[b, 2 * count : 2 * count + CODE_ROWS, 0:count] for b in range(blocks)]
    chosen, shares = selections(tiles, arm.astype(F32), capacity)
    for b in range(blocks):
        at = slice(b * capacity, (b + 1) * capacity)
        rows[at] = mm(chosen[b], held[b, 0:count]).astype(BF16)
        cots[at] = (mm(chosen[b], held[b, count : 2 * count]) * shares[b]).astype(BF16)

    for load in loads[blocks : blocks + 3]:
        load.wait()
    for k in range(pieces):
        piece = hid.shape[2]
        cut = slice(k * piece, (k + 1) * piece)
        gate_pre = mm(rows[...], gate_ref[:, cut])
        up_pre = mm(rows[...], up_ref[:, cut])
        d_hidden = mm_nt(cots[...], down_ref[cut, :])
        sig = 0.5 * jnp.tanh(0.5 * gate_pre) + 0.5
        activated = gate_pre * sig
        hid[k] = (activated * up_pre).astype(BF16)
        dup[k] = (d_hidden * activated).astype(BF16)
        dgate[k] = (d_hidden * up_pre * (sig + activated * (1.0 - sig))).astype(BF16)
    if not saved:
        for store in stores[2:]:
            store.start()

    total_out, total_in = None, None
    for k in range(pieces):
        cut = slice(k * piece, (k + 1) * piece)
        out_part = mm(hid[k], down_ref[cut, :])
        in_part = mm_nt(dgate[k], gate_ref[:, cut]) + mm_nt(dup[k], up_ref[:, cut])
        total_out = out_part if k == 0 else total_out + out_part
        total_in = in_part if k == 0 else total_in + in_part
    for b in range(blocks):
        at = slice(b * capacity, (b + 1) * capacity)
        target = keep_ref if b < blocks // 2 else give_ref
        out_rows = (total_out[at].astype(BF16).astype(F32) * shares[b]).astype(BF16)
        target[b % (blocks // 2), 0] = mm_tn(chosen[b], out_rows).astype(BF16)
        in_rows = total_in[at].astype(BF16)
        target[b % (blocks // 2), 1] = mm_tn(chosen[b], in_rows).astype(BF16)
    stores[0].start()
    stores[1].start()

    if saved:
        for load in loads[blocks + 3 :]:
            load.wait()
        parts = staged[2:]
        all_rows = jnp.concatenate([saved[0][...], rows[...]], axis=0)
        all_cots = jnp.concatenate([saved[1][...], cots[...]], axis=0)
        half = all_rows.shape[1] // 2
        x_ref, y_ref, x_next_ref, y_next_ref, first_ref, second_ref = parts
        plan = (
            (3, x_ref.at[0], y_ref.at[0], ()),
            (1, x_ref.at[1], x_next_ref, (0, 2)),
            (2, y_next_ref, y_ref.at[1], (1, 3)),
            (0, first_ref, second_ref, (4, 5)),
        )
        for j, first, second, complete in plan:
            quarter = place ^ j
            both = lambda old, new: jnp.concatenate([old[quarter], new[quarter]], axis=0)
            for k, d_pre in enumerate((both(saved[3], dgate), both(saved[4], dup))):
                part = mm_tn(all_rows, d_pre).astype(BF16)
                first[k] = part[:half]
                second[k] = part[half:]
            part = mm_tn(both(saved[2], hid), all_cots).astype(BF16)
            first[2] = part[:, :half]
            second[2] = part[:, half:]
            for n in complete:
                stores[2 + n].start()
    for store in stores:
        store.wait()


def finish_kernel(*refs):
    gate_ref, up_ref, down_ref = refs[6:]
    half = gate_ref.shape[0] // 2
    for k in (0, 1):
        mine, got, late = refs[3 * k : 3 * k + 3]
        total = mine[...].astype(F32) + got[1].astype(F32) + late[...].astype(F32)
        total = total.astype(BF16)
        at = slice(k * half, (k + 1) * half)
        gate_ref[at] = total[0]
        up_ref[at] = total[1]
        down_ref[:, at] = total[2]


def vmem():
    return pl.BlockSpec(memory_space=pltpu.VMEM)


def run_pack(tokens, cotangent, codes):
    count, width = tokens.shape
    return pl.pallas_call(
        pack_kernel,
        in_specs=[vmem()] * 3,
        out_specs=vmem(),
        out_shape=jax.ShapeDtypeStruct((2 * count + CODE_ROWS, width), BF16),
        name="pack",
    )(tokens, cotangent, codes.T)


def run_arm(parts, capacity, weights, piece, saved=()):
    blocks = len(parts)
    width, hidden_width = weights[0].shape
    count = (parts[0].shape[0] - CODE_ROWS) // 2
    rows = blocks * capacity
    pieces = hidden_width // piece
    one = (3, width // 2, piece)
    made = [(rows, width)] * 2 + [(pieces, rows, piece)] * 3
    outs = [(blocks // 2, 2, count, width)] * 2
    outs += [(2,) + one] * 2 + [one] * 4 if saved else made
    held = [(blocks,) + parts[0].shape] + [weight.shape for weight in weights]
    held += [array.shape for array in saved] + made if saved else []
    sources = (*parts, *weights, *saved)
    anywhere = pl.BlockSpec(memory_space=pl.ANY)
    return pl.pallas_call(
        functools.partial(arm_kernel, blocks, len(sources), len(outs)),
        in_specs=[anywhere] * len(sources),
        out_specs=[anywhere] * len(outs),
        out_shape=[jax.ShapeDtypeStruct(shape, BF16) for shape in outs],
        scratch_shapes=[pltpu.VMEM(shape, BF16) for shape in held + outs]
        + [
            pltpu.SemaphoreType.DMA((len(sources),)),
            pltpu.SemaphoreType.DMA((len(outs),)),
        ],
        compiler_params=pltpu.CompilerParams(vmem_limit_bytes=VMEM_BYTES),
        cost_estimate=pl.CostEstimate(
            flops=(24 if saved else 12) * rows * width * hidden_width,
            bytes_accessed=12 << 20,
            transcendentals=0,
        ),
        name="arm_late" if saved else "arm_early",
    )(*sources)


def run_finish(*parts):
    _, half, share = parts[0].shape
    width = 2 * half
    outs = [(width, share), (width, share), (share, width)]
    return pl.pallas_call(
        finish_kernel,
        in_specs=[vmem()] * 6,
        out_specs=[vmem()] * 3,
        out_shape=[jax.ShapeDtypeStruct(shape, BF16) for shape in outs],
        compiler_params=pltpu.CompilerParams(vmem_limit_bytes=8 * 1024 * 1024),
        name="finish",
    )(*parts)


def on_line(tokens, codes, cotangent, w_gate, w_up, w_down):
    token_count, width = tokens.shape
    arm_count = lax.axis_size("expert")
    capacity = 4 * token_count // arm_count
    w_gate, w_up, w_down = w_gate[0], w_up[0], w_down[0]
    hidden_width = w_gate.shape[1]
    chunk = hidden_width // lax.axis_size("dp")
    z = lax.axis_index("expert") // 2
    edge = (z == 0) | (z == 3)

    def along(pairs):
        return [(2 * s + c, 2 * d + c) for s, d in pairs for c in (0, 1)]

    far = along([(0, 3), (3, 0), (1, 2), (2, 1)])
    near = along([(0, 1), (1, 0), (2, 3), (3, 2)])
    skip = along([(0, 2), (2, 3), (3, 1), (1, 0)])
    skip_back = along([(2, 0), (3, 2), (1, 3), (0, 1)])
    core = [(e, e ^ 1) for e in range(8)]
    x_pair = [(i, i ^ 1) for i in range(4)]
    y_pair = [(i, i ^ 2) for i in range(4)]
    send = lambda value, pairs: lax.ppermute(value, "expert", pairs)
    send_dp = lambda value, pairs: lax.ppermute(value, "dp", pairs)

    own = run_pack(tokens, cotangent, codes)
    add = lambda a, b: a.astype(F32) + b.astype(F32)
    run = functools.partial(
        run_arm,
        capacity=capacity,
        weights=(w_gate, w_up, w_down),
        piece=chunk,
    )
    from_far = send(own, far)
    from_near = send(own, near)
    keep, give, *saved = run([own, from_near, send(own, core), send(from_near, core)])
    from_skip = send(jnp.where(edge, own, from_far), skip)
    from_skip, keep = lax.optimization_barrier((from_skip, keep))
    got = send(give, core)
    for_own = add(keep[0], got[0])
    for_near = add(keep[1], got[1]).astype(BF16)
    keep, give, x_part, y_part, x_next, y_next, k0, k1 = run(
        [from_far, from_skip, send(from_far, core), send(from_skip, core)], saved=saved
    )
    got = send(give, core)
    for_far = add(keep[0], got[0])
    for_skip = add(keep[1], got[1]).astype(BF16)
    from_x, from_y = send_dp(x_part, x_pair), send_dp(y_part, y_pair)
    from_skip = send(for_skip, skip_back).astype(F32)
    from_near = send(for_near, near)
    for_far = for_far + jnp.where(edge, 0.0, from_skip)
    from_far = send(for_far.astype(BF16), far)
    result = for_own + from_near + from_far + jnp.where(edge, from_skip, 0.0)
    head_output, grad_tokens = result[0].astype(BF16), result[1].astype(BF16)

    y_next = add(y_next, from_x[0]).astype(BF16)
    x_next = add(x_next, from_y[0]).astype(BF16)
    grads = run_finish(
        k0, from_x, send_dp(y_next, y_pair), k1, from_y, send_dp(x_next, x_pair)
    )
    grad_gate, grad_up, grad_down = (part[None] for part in grads)
    return (head_output, grad_tokens, grad_gate, grad_up, grad_down)


def solution(mesh):
    on_square_of_lines = mesh.shape["dp"] == 4 and mesh.shape["expert"] == 8
    return jax.shard_map(
        on_line if on_square_of_lines else on_device,
        mesh=mesh,
        in_specs=(
            P(("dp", "expert"), None),
            P(("dp", "expert"), None),
            P(("dp", "expert"), None),
            P("expert", None, None),
            P("expert", None, None),
            P("expert", None, None),
        ),
        out_specs=(
            P(("dp", "expert"), None),
            P(("dp", "expert"), None),
            P("expert", None, "dp"),
            P("expert", None, "dp"),
            P("expert", "dp", None),
        ),
        check_vma=False,
    )
```

```python
import functools

import jax
import jax.numpy as jnp
from jax import lax
from jax.experimental import pallas as pl
from jax.experimental.pallas import tpu as pltpu
from jax.sharding import PartitionSpec as P

fact_share = 0.7
counter_share = 0.3

F32 = jnp.float32
BF16 = jnp.bfloat16
CODE_ROWS = 16
VMEM_BYTES = 16 * 1024 * 1024

def rounded(value):
    return lax.optimization_barrier(value.astype(jnp.bfloat16)).astype(jnp.float32)


def silu_parts(gate_pre):
    sigmoid_gate = jax.nn.sigmoid(gate_pre)
    return (gate_pre * sigmoid_gate, sigmoid_gate * (1.0 + gate_pre * (1.0 - sigmoid_gate)))


def arm_forward(rows_in, gate_w, up_w):
    gate_pre = jnp.einsum("arc,ach->arh", rows_in, gate_w, preferred_element_type=jnp.float32)
    up_pre = jnp.einsum("arc,ach->arh", rows_in, up_w, preferred_element_type=jnp.float32)
    activated, silu_slope = silu_parts(gate_pre)
    hidden = (activated * up_pre).astype(jnp.bfloat16)
    return (up_pre, activated, silu_slope, hidden)


def arm_backward(up_pre, activated, silu_slope, cot_in, down_w):
    d_hidden = jnp.einsum("arc,ahc->arh", cot_in, down_w, preferred_element_type=jnp.float32)
    d_up = (d_hidden * activated).astype(jnp.bfloat16)
    d_gate = (d_hidden * up_pre * silu_slope).astype(jnp.bfloat16)
    return (d_gate, d_up)


def on_device(tokens, codes, cotangent, w_gate, w_up, w_down):
    token_count, feature_width = tokens.shape
    local_arms = w_gate.shape[0]
    arm_count = local_arms * lax.axis_size("expert")
    capacity = 4 * token_count // arm_count
    flat_codes = codes.reshape(-1)
    arm_ids = jnp.arange(arm_count, dtype=jnp.int32)
    onehot = (flat_codes[:, None] == arm_ids[None, :]).astype(jnp.int32)
    earlier = jnp.cumsum(onehot, axis=0) - onehot
    destination = flat_codes * capacity + jnp.sum(earlier * onehot, axis=1)
    shares = jnp.tile(jnp.array([fact_share, counter_share], jnp.float32), token_count)
    token_rows = jnp.repeat(tokens, 2, axis=0)
    cot_rows = (jnp.repeat(cotangent.astype(jnp.float32), 2, axis=0) * shares[:, None]).astype(
        jnp.bfloat16
    )
    blank_rows = jnp.zeros((arm_count * capacity, feature_width), jnp.bfloat16)
    send_tokens = (
        blank_rows.at[destination].set(token_rows).reshape(arm_count, capacity, feature_width)
    )
    send_cot = blank_rows.at[destination].set(cot_rows).reshape(arm_count, capacity, feature_width)
    arm_tokens, arm_cot = (
        lax.all_to_all(send_tokens, "expert", split_axis=0, concat_axis=1, tiled=True),
        lax.all_to_all(send_cot, "expert", split_axis=0, concat_axis=1, tiled=True),
    )
    up_pre, activated, silu_slope, hidden = arm_forward(arm_tokens, w_gate, w_up)
    out_rows = jnp.einsum(
        "arh,ahc->arc", hidden, w_down, preferred_element_type=jnp.float32
    ).astype(jnp.bfloat16)
    d_gate, d_up = arm_backward(up_pre, activated, silu_slope, arm_cot, w_down)
    input_rows = (
        jnp.einsum("arh,ach->arc", d_gate, w_gate, preferred_element_type=jnp.float32)
        + jnp.einsum("arh,ach->arc", d_up, w_up, preferred_element_type=jnp.float32)
    ).astype(jnp.bfloat16)
    back_out, back_input = (
        lax.all_to_all(out_rows, "expert", split_axis=1, concat_axis=0, tiled=True),
        lax.all_to_all(input_rows, "expert", split_axis=1, concat_axis=0, tiled=True),
    )
    back_out = back_out.reshape(arm_count * capacity, feature_width)[destination]
    back_out = back_out.reshape(token_count, 2, feature_width).astype(jnp.float32)
    back_input = back_input.reshape(arm_count * capacity, feature_width)[destination]
    back_input = back_input.reshape(token_count, 2, feature_width).astype(jnp.float32)
    head_output = (fact_share * back_out[:, 0] + counter_share * back_out[:, 1]).astype(
        jnp.bfloat16
    )
    grad_tokens = (back_input[:, 0] + back_input[:, 1]).astype(jnp.bfloat16)
    all_tokens, all_cot = (
        lax.all_gather(arm_tokens, "dp", axis=1, tiled=True),
        lax.all_gather(arm_cot, "dp", axis=1, tiled=True),
    )
    group_count = lax.axis_size("dp")
    hidden_width = w_gate.shape[2]
    quarter = hidden_width // group_count
    first_unit = lax.axis_index("dp") * quarter
    gate_share = lax.dynamic_slice_in_dim(w_gate, first_unit, quarter, 2)
    up_share = lax.dynamic_slice_in_dim(w_up, first_unit, quarter, 2)
    down_share = lax.dynamic_slice_in_dim(w_down, first_unit, quarter, 1)
    row_count = arm_tokens.shape[1]
    total_gate = jnp.zeros((local_arms, feature_width, quarter), jnp.float32)
    total_up = jnp.zeros((local_arms, feature_width, quarter), jnp.float32)
    total_down = jnp.zeros((local_arms, quarter, feature_width), jnp.float32)
    for group_index in range(group_count):
        some_tokens = all_tokens[:, group_index * row_count : (group_index + 1) * row_count]
        some_cot = all_cot[:, group_index * row_count : (group_index + 1) * row_count]
        piece_up, piece_act, piece_slope, piece_hidden = arm_forward(
            some_tokens, gate_share, up_share
        )
        piece_dgate, piece_dup = arm_backward(
            piece_up, piece_act, piece_slope, some_cot, down_share
        )
        total_gate = total_gate + rounded(
            jnp.einsum("arc,arh->ach", some_tokens, piece_dgate, preferred_element_type=jnp.float32)
        )
        total_up = total_up + rounded(
            jnp.einsum("arc,arh->ach", some_tokens, piece_dup, preferred_element_type=jnp.float32)
        )
        total_down = total_down + rounded(
            jnp.einsum("arh,arc->ahc", piece_hidden, some_cot, preferred_element_type=jnp.float32)
        )
    grad_gate = total_gate.astype(jnp.bfloat16)
    grad_up = total_up.astype(jnp.bfloat16)
    grad_down = total_down.astype(jnp.bfloat16)
    return (head_output, grad_tokens, grad_gate, grad_up, grad_down)


def mm(left, right):
    return jnp.dot(left, right, preferred_element_type=F32)


def mm_nt(left, right):
    return lax.dot_general(left, right, (((1,), (1,)), ((), ())), preferred_element_type=F32)


def mm_tn(left, right):
    return lax.dot_general(left, right, (((0,), (0,)), ((), ())), preferred_element_type=F32)


def selections(code_tiles, arm, capacity):
    count = code_tiles[0].shape[1]
    named = [(tile.astype(F32) == arm).astype(F32) for tile in code_tiles]
    before = lax.broadcasted_iota(jnp.int32, (count, count), 0)
    after = lax.broadcasted_iota(jnp.int32, (count, count), 1)
    ranks = mm(jnp.concatenate(named, axis=0).astype(BF16), (before < after).astype(BF16))
    slot = lax.broadcasted_iota(jnp.int32, (capacity, count), 0).astype(F32)
    chosen, shares = [], []
    for b, hit in enumerate(named):
        rank = ranks[b * CODE_ROWS : b * CODE_ROWS + 1] + ranks[b * CODE_ROWS + 1 : b * CODE_ROWS + 2]
        here = jnp.where(slot == rank, hit[0:1] + hit[1:2], 0.0)
        share = fact_share * hit[0:1] + counter_share * hit[1:2]
        chosen.append(here.astype(BF16))
        shares.append(jnp.sum(here * share, axis=1, keepdims=True))
    return chosen, shares


def pack_kernel(tokens_ref, cot_ref, codes_ref, out_ref):
    count = tokens_ref.shape[0]
    out_ref[0:count] = tokens_ref[...]
    out_ref[count : 2 * count] = cot_ref[...]
    out_ref[2 * count : 2 * count + CODE_ROWS] = jnp.zeros((CODE_ROWS, out_ref.shape[1]), BF16)
    rows = lax.broadcasted_iota(jnp.int32, (CODE_ROWS, count), 0)
    codes = codes_ref[...].astype(F32)
    both = jnp.where(rows == 0, codes[0:1], jnp.where(rows == 1, codes[1:2], 0.0))
    out_ref[2 * count : 2 * count + CODE_ROWS, 0:count] = both.astype(BF16)


def arm_kernel(blocks, outs_count, *refs):
    held, refs = refs[:blocks], refs[blocks:]
    (gate_ref, up_ref, down_ref), refs = refs[:3], refs[3:]
    saved, refs = (refs[:5], refs[5:]) if outs_count == 8 else ((), refs)
    staged, made = refs[:outs_count], refs[outs_count:]
    keep_ref, give_ref = staged[:2]
    rows, cots, hid, dgate, dup = made if saved else staged[2:]
    capacity, count = rows.shape[0] // blocks, keep_ref.shape[2]
    pieces = hid.shape[0]
    arm, place = lax.axis_index("expert"), lax.axis_index("dp")

    tiles = [ref[2 * count : 2 * count + CODE_ROWS, 0:count] for ref in held]
    chosen, shares = selections(tiles, arm.astype(F32), capacity)
    for b in range(blocks):
        at = slice(b * capacity, (b + 1) * capacity)
        rows[at] = mm(chosen[b], held[b][0:count]).astype(BF16)
        picked = mm(chosen[b], held[b][count : 2 * count])
        cots[at] = (picked * shares[b]).astype(BF16)

    for k in range(pieces):
        piece = hid.shape[2]
        cut = slice(k * piece, (k + 1) * piece)
        gate_pre = mm(rows[...], gate_ref[:, cut])
        up_pre = mm(rows[...], up_ref[:, cut])
        d_hidden = mm_nt(cots[...], down_ref[cut, :])
        sig = 0.5 * jnp.tanh(0.5 * gate_pre) + 0.5
        activated = gate_pre * sig
        hid[k] = (activated * up_pre).astype(BF16)
        dup[k] = (d_hidden * activated).astype(BF16)
        dgate[k] = (d_hidden * up_pre * (sig + activated * (1.0 - sig))).astype(BF16)

    total_out, total_in = None, None
    for k in range(pieces):
        cut = slice(k * piece, (k + 1) * piece)
        out_part = mm(hid[k], down_ref[cut, :])
        in_part = mm_nt(dgate[k], gate_ref[:, cut]) + mm_nt(dup[k], up_ref[:, cut])
        total_out = out_part if k == 0 else total_out + out_part
        total_in = in_part if k == 0 else total_in + in_part
    for b in range(blocks):
        at = slice(b * capacity, (b + 1) * capacity)
        target = keep_ref if b < blocks // 2 else give_ref
        out_rows = (total_out[at].astype(BF16).astype(F32) * shares[b]).astype(BF16)
        target[b % (blocks // 2), 0] = mm_tn(chosen[b], out_rows).astype(BF16)
        in_rows = total_in[at].astype(BF16)
        target[b % (blocks // 2), 1] = mm_tn(chosen[b], in_rows).astype(BF16)

    if saved:
        parts = staged[2:]
        all_rows = jnp.concatenate([saved[0][...], rows[...]], axis=0)
        all_cots = jnp.concatenate([saved[1][...], cots[...]], axis=0)
        half = all_rows.shape[1] // 2
        x_ref, y_ref, x_next_ref, y_next_ref, first_ref, second_ref = parts
        plan = (
            (3, x_ref.at[0], y_ref.at[0]),
            (1, x_ref.at[1], x_next_ref),
            (2, y_next_ref, y_ref.at[1]),
            (0, first_ref, second_ref),
        )
        for j, first, second in plan:
            quarter = place ^ j
            both = lambda old, new: jnp.concatenate([old[quarter], new[quarter]], axis=0)
            for k, d_pre in enumerate((both(saved[3], dgate), both(saved[4], dup))):
                part = mm_tn(all_rows, d_pre).astype(BF16)
                first[k] = part[:half]
                second[k] = part[half:]
            part = mm_tn(both(saved[2], hid), all_cots).astype(BF16)
            first[2] = part[:, :half]
            second[2] = part[:, half:]


def finish_kernel(*refs):
    gate_ref, up_ref, down_ref = refs[6:]
    half = gate_ref.shape[0] // 2
    for k in (0, 1):
        mine, got, late = refs[3 * k : 3 * k + 3]
        total = mine[...].astype(F32) + got[1].astype(F32) + late[...].astype(F32)
        total = total.astype(BF16)
        at = slice(k * half, (k + 1) * half)
        gate_ref[at] = total[0]
        up_ref[at] = total[1]
        down_ref[:, at] = total[2]


def vmem():
    return pl.BlockSpec(memory_space=pltpu.VMEM)


def run_pack(tokens, cotangent, codes):
    count, width = tokens.shape
    return pl.pallas_call(
        pack_kernel,
        in_specs=[vmem()] * 3,
        out_specs=vmem(),
        out_shape=jax.ShapeDtypeStruct((2 * count + CODE_ROWS, width), BF16),
        compiler_params=pltpu.CompilerParams(vmem_limit_bytes=4 * 1024 * 1024),
        name="pack",
    )(tokens, cotangent, codes.T)


def run_arm(parts, capacity, weights, piece, saved=()):
    blocks = len(parts)
    width, hidden_width = weights[0].shape
    count = (parts[0].shape[0] - CODE_ROWS) // 2
    rows = blocks * capacity
    pieces = hidden_width // piece
    one = (3, width // 2, piece)
    made = [(rows, width)] * 2 + [(pieces, rows, piece)] * 3
    outs = [(blocks // 2, 2, count, width)] * 2
    outs += [(2,) + one] * 2 + [one] * 4 if saved else made
    ins = (*parts, *weights, *saved)
    return pl.pallas_call(
        functools.partial(arm_kernel, blocks, len(outs)),
        in_specs=[vmem()] * len(ins),
        out_specs=[vmem()] * len(outs),
        out_shape=[jax.ShapeDtypeStruct(shape, BF16) for shape in outs],
        scratch_shapes=[pltpu.VMEM(shape, BF16) for shape in made] if saved else [],
        compiler_params=pltpu.CompilerParams(vmem_limit_bytes=VMEM_BYTES),
        cost_estimate=pl.CostEstimate(
            flops=(24 if saved else 12) * rows * width * hidden_width,
            bytes_accessed=12 << 20,
            transcendentals=0,
        ),
        name="arm_late" if saved else "arm_early",
    )(*ins)


def run_finish(*parts):
    _, half, share = parts[0].shape
    width = 2 * half
    outs = [(width, share), (width, share), (share, width)]
    return pl.pallas_call(
        finish_kernel,
        in_specs=[vmem()] * 6,
        out_specs=[vmem()] * 3,
        out_shape=[jax.ShapeDtypeStruct(shape, BF16) for shape in outs],
        compiler_params=pltpu.CompilerParams(vmem_limit_bytes=8 * 1024 * 1024),
        name="finish",
    )(*parts)


def on_line(tokens, codes, cotangent, w_gate, w_up, w_down):
    token_count, width = tokens.shape
    arm_count = lax.axis_size("expert")
    capacity = 4 * token_count // arm_count
    w_gate, w_up, w_down = w_gate[0], w_up[0], w_down[0]
    hidden_width = w_gate.shape[1]
    chunk = hidden_width // lax.axis_size("dp")
    z = lax.axis_index("expert") // 2
    edge = (z == 0) | (z == 3)

    def along(pairs):
        return [(2 * s + c, 2 * d + c) for s, d in pairs for c in (0, 1)]

    far = along([(0, 3), (3, 0), (1, 2), (2, 1)])
    near = along([(0, 1), (1, 0), (2, 3), (3, 2)])
    skip = along([(0, 2), (2, 3), (3, 1), (1, 0)])
    skip_back = along([(2, 0), (3, 2), (1, 3), (0, 1)])
    core = [(e, e ^ 1) for e in range(8)]
    x_pair = [(i, i ^ 1) for i in range(4)]
    y_pair = [(i, i ^ 2) for i in range(4)]
    send = lambda value, pairs: lax.ppermute(value, "expert", pairs)
    send_dp = lambda value, pairs: lax.ppermute(value, "dp", pairs)

    own = run_pack(tokens, cotangent, codes)
    add = lambda a, b: a.astype(F32) + b.astype(F32)
    run = functools.partial(
        run_arm,
        capacity=capacity,
        weights=(w_gate, w_up, w_down),
        piece=chunk,
    )
    from_far = send(own, far)
    from_near = send(own, near)
    keep, give, *saved = run([own, from_near, send(own, core), send(from_near, core)])
    from_skip = send(jnp.where(edge, own, from_far), skip)
    from_skip, keep = lax.optimization_barrier((from_skip, keep))
    got = send(give, core)
    for_own = add(keep[0], got[0])
    for_near = add(keep[1], got[1]).astype(BF16)
    keep, give, x_part, y_part, x_next, y_next, k0, k1 = run(
        [from_far, from_skip, send(from_far, core), send(from_skip, core)], saved=saved
    )
    got = send(give, core)
    for_far = add(keep[0], got[0])
    for_skip = add(keep[1], got[1]).astype(BF16)
    from_x, from_y = send_dp(x_part, x_pair), send_dp(y_part, y_pair)
    from_skip = send(for_skip, skip_back).astype(F32)
    from_near = send(for_near, near)
    for_far = for_far + jnp.where(edge, 0.0, from_skip)
    from_far = send(for_far.astype(BF16), far)
    result = for_own + from_near + from_far + jnp.where(edge, from_skip, 0.0)
    head_output, grad_tokens = result[0].astype(BF16), result[1].astype(BF16)

    y_next = add(y_next, from_x[0]).astype(BF16)
    x_next = add(x_next, from_y[0]).astype(BF16)
    grads = run_finish(
        k0, from_x, send_dp(y_next, y_pair), k1, from_y, send_dp(x_next, x_pair)
    )
    grad_gate, grad_up, grad_down = (part[None] for part in grads)
    return (head_output, grad_tokens, grad_gate, grad_up, grad_down)


def solution(mesh):
    on_square_of_lines = mesh.shape["dp"] == 4 and mesh.shape["expert"] == 8
    return jax.shard_map(
        on_line if on_square_of_lines else on_device,
        mesh=mesh,
        in_specs=(
            P(("dp", "expert"), None),
            P(("dp", "expert"), None),
            P(("dp", "expert"), None),
            P("expert", None, None),
            P("expert", None, None),
            P("expert", None, None),
        ),
        out_specs=(
            P(("dp", "expert"), None),
            P(("dp", "expert"), None),
            P("expert", None, "dp"),
            P("expert", None, "dp"),
            P("expert", "dp", None),
        ),
        check_vma=False,
    )
```

```python
import functools

import jax
import jax.numpy as jnp
from jax import lax
from jax.experimental import pallas as pl
from jax.experimental.pallas import tpu as pltpu
from jax.sharding import PartitionSpec as P

fact_share = 0.7
counter_share = 0.3

F32 = jnp.float32
BF16 = jnp.bfloat16
CODE_ROWS = 16
VMEM_BYTES = 16 * 1024 * 1024

def rounded(value):
    return lax.optimization_barrier(value.astype(jnp.bfloat16)).astype(jnp.float32)


def silu_parts(gate_pre):
    sigmoid_gate = jax.nn.sigmoid(gate_pre)
    return (gate_pre * sigmoid_gate, sigmoid_gate * (1.0 + gate_pre * (1.0 - sigmoid_gate)))


def arm_forward(rows_in, gate_w, up_w):
    gate_pre = jnp.einsum("arc,ach->arh", rows_in, gate_w, preferred_element_type=jnp.float32)
    up_pre = jnp.einsum("arc,ach->arh", rows_in, up_w, preferred_element_type=jnp.float32)
    activated, silu_slope = silu_parts(gate_pre)
    hidden = (activated * up_pre).astype(jnp.bfloat16)
    return (up_pre, activated, silu_slope, hidden)


def arm_backward(up_pre, activated, silu_slope, cot_in, down_w):
    d_hidden = jnp.einsum("arc,ahc->arh", cot_in, down_w, preferred_element_type=jnp.float32)
    d_up = (d_hidden * activated).astype(jnp.bfloat16)
    d_gate = (d_hidden * up_pre * silu_slope).astype(jnp.bfloat16)
    return (d_gate, d_up)


def on_device(tokens, codes, cotangent, w_gate, w_up, w_down):
    token_count, feature_width = tokens.shape
    local_arms = w_gate.shape[0]
    arm_count = local_arms * lax.axis_size("expert")
    capacity = 4 * token_count // arm_count
    flat_codes = codes.reshape(-1)
    arm_ids = jnp.arange(arm_count, dtype=jnp.int32)
    onehot = (flat_codes[:, None] == arm_ids[None, :]).astype(jnp.int32)
    earlier = jnp.cumsum(onehot, axis=0) - onehot
    destination = flat_codes * capacity + jnp.sum(earlier * onehot, axis=1)
    shares = jnp.tile(jnp.array([fact_share, counter_share], jnp.float32), token_count)
    token_rows = jnp.repeat(tokens, 2, axis=0)
    cot_rows = (jnp.repeat(cotangent.astype(jnp.float32), 2, axis=0) * shares[:, None]).astype(
        jnp.bfloat16
    )
    blank_rows = jnp.zeros((arm_count * capacity, feature_width), jnp.bfloat16)
    send_tokens = (
        blank_rows.at[destination].set(token_rows).reshape(arm_count, capacity, feature_width)
    )
    send_cot = blank_rows.at[destination].set(cot_rows).reshape(arm_count, capacity, feature_width)
    arm_tokens, arm_cot = (
        lax.all_to_all(send_tokens, "expert", split_axis=0, concat_axis=1, tiled=True),
        lax.all_to_all(send_cot, "expert", split_axis=0, concat_axis=1, tiled=True),
    )
    up_pre, activated, silu_slope, hidden = arm_forward(arm_tokens, w_gate, w_up)
    out_rows = jnp.einsum(
        "arh,ahc->arc", hidden, w_down, preferred_element_type=jnp.float32
    ).astype(jnp.bfloat16)
    d_gate, d_up = arm_backward(up_pre, activated, silu_slope, arm_cot, w_down)
    input_rows = (
        jnp.einsum("arh,ach->arc", d_gate, w_gate, preferred_element_type=jnp.float32)
        + jnp.einsum("arh,ach->arc", d_up, w_up, preferred_element_type=jnp.float32)
    ).astype(jnp.bfloat16)
    back_out, back_input = (
        lax.all_to_all(out_rows, "expert", split_axis=1, concat_axis=0, tiled=True),
        lax.all_to_all(input_rows, "expert", split_axis=1, concat_axis=0, tiled=True),
    )
    back_out = back_out.reshape(arm_count * capacity, feature_width)[destination]
    back_out = back_out.reshape(token_count, 2, feature_width).astype(jnp.float32)
    back_input = back_input.reshape(arm_count * capacity, feature_width)[destination]
    back_input = back_input.reshape(token_count, 2, feature_width).astype(jnp.float32)
    head_output = (fact_share * back_out[:, 0] + counter_share * back_out[:, 1]).astype(
        jnp.bfloat16
    )
    grad_tokens = (back_input[:, 0] + back_input[:, 1]).astype(jnp.bfloat16)
    all_tokens, all_cot = (
        lax.all_gather(arm_tokens, "dp", axis=1, tiled=True),
        lax.all_gather(arm_cot, "dp", axis=1, tiled=True),
    )
    group_count = lax.axis_size("dp")
    hidden_width = w_gate.shape[2]
    quarter = hidden_width // group_count
    first_unit = lax.axis_index("dp") * quarter
    gate_share = lax.dynamic_slice_in_dim(w_gate, first_unit, quarter, 2)
    up_share = lax.dynamic_slice_in_dim(w_up, first_unit, quarter, 2)
    down_share = lax.dynamic_slice_in_dim(w_down, first_unit, quarter, 1)
    row_count = arm_tokens.shape[1]
    total_gate = jnp.zeros((local_arms, feature_width, quarter), jnp.float32)
    total_up = jnp.zeros((local_arms, feature_width, quarter), jnp.float32)
    total_down = jnp.zeros((local_arms, quarter, feature_width), jnp.float32)
    for group_index in range(group_count):
        some_tokens = all_tokens[:, group_index * row_count : (group_index + 1) * row_count]
        some_cot = all_cot[:, group_index * row_count : (group_index + 1) * row_count]
        piece_up, piece_act, piece_slope, piece_hidden = arm_forward(
            some_tokens, gate_share, up_share
        )
        piece_dgate, piece_dup = arm_backward(
            piece_up, piece_act, piece_slope, some_cot, down_share
        )
        total_gate = total_gate + rounded(
            jnp.einsum("arc,arh->ach", some_tokens, piece_dgate, preferred_element_type=jnp.float32)
        )
        total_up = total_up + rounded(
            jnp.einsum("arc,arh->ach", some_tokens, piece_dup, preferred_element_type=jnp.float32)
        )
        total_down = total_down + rounded(
            jnp.einsum("arh,arc->ahc", piece_hidden, some_cot, preferred_element_type=jnp.float32)
        )
    grad_gate = total_gate.astype(jnp.bfloat16)
    grad_up = total_up.astype(jnp.bfloat16)
    grad_down = total_down.astype(jnp.bfloat16)
    return (head_output, grad_tokens, grad_gate, grad_up, grad_down)


def mm(left, right):
    return jnp.dot(left, right, preferred_element_type=F32)


def mm_nt(left, right):
    return lax.dot_general(left, right, (((1,), (1,)), ((), ())), preferred_element_type=F32)


def mm_tn(left, right):
    return lax.dot_general(left, right, (((0,), (0,)), ((), ())), preferred_element_type=F32)


def selections(code_tiles, arm, capacity):
    count = code_tiles[0].shape[1]
    named = [(tile.astype(F32) == arm).astype(F32) for tile in code_tiles]
    before = lax.broadcasted_iota(jnp.int32, (count, count), 0)
    after = lax.broadcasted_iota(jnp.int32, (count, count), 1)
    ranks = mm(jnp.concatenate(named, axis=0).astype(BF16), (before < after).astype(BF16))
    slot = lax.broadcasted_iota(jnp.int32, (capacity, count), 0).astype(F32)
    chosen, shares = [], []
    for b, hit in enumerate(named):
        rank = ranks[b * CODE_ROWS : b * CODE_ROWS + 1] + ranks[b * CODE_ROWS + 1 : b * CODE_ROWS + 2]
        here = jnp.where(slot == rank, hit[0:1] + hit[1:2], 0.0)
        share = fact_share * hit[0:1] + counter_share * hit[1:2]
        chosen.append(here.astype(BF16))
        shares.append(jnp.sum(here * share, axis=1, keepdims=True))
    return chosen, shares


def pack_kernel(tokens_ref, cot_ref, codes_ref, out_ref):
    count = tokens_ref.shape[0]
    out_ref[0:count] = tokens_ref[...]
    out_ref[count : 2 * count] = cot_ref[...]
    out_ref[2 * count : 2 * count + CODE_ROWS] = jnp.zeros((CODE_ROWS, out_ref.shape[1]), BF16)
    rows = lax.broadcasted_iota(jnp.int32, (CODE_ROWS, count), 0)
    codes = codes_ref[...].astype(F32)
    both = jnp.where(rows == 0, codes[0:1], jnp.where(rows == 1, codes[1:2], 0.0))
    out_ref[2 * count : 2 * count + CODE_ROWS, 0:count] = both.astype(BF16)


def arm_kernel(blocks, outs_count, *refs):
    held, refs = refs[:blocks], refs[blocks:]
    (gate_ref, up_ref, down_ref), refs = refs[:3], refs[3:]
    saved, refs = (refs[:5], refs[5:]) if outs_count == 10 else ((), refs)
    staged, made = refs[:outs_count], refs[outs_count:]
    keep_ref, give_ref = staged[:2]
    rows, cots, hid, dgate, dup = made if saved else staged[2:]
    capacity, count = rows.shape[0] // blocks, keep_ref.shape[2]
    pieces = hid.shape[0]
    arm, place = lax.axis_index("expert"), lax.axis_index("dp")

    tiles = [ref[2 * count : 2 * count + CODE_ROWS, 0:count] for ref in held]
    chosen, shares = selections(tiles, arm.astype(F32), capacity)
    for b in range(blocks):
        at = slice(b * capacity, (b + 1) * capacity)
        rows[at] = mm(chosen[b], held[b][0:count]).astype(BF16)
        picked = mm(chosen[b], held[b][count : 2 * count])
        cots[at] = (picked * shares[b]).astype(BF16)

    for k in range(pieces):
        piece = hid.shape[2]
        cut = slice(k * piece, (k + 1) * piece)
        gate_pre = mm(rows[...], gate_ref[:, cut])
        up_pre = mm(rows[...], up_ref[:, cut])
        d_hidden = mm_nt(cots[...], down_ref[cut, :])
        sig = 0.5 * jnp.tanh(0.5 * gate_pre) + 0.5
        activated = gate_pre * sig
        hid[k] = (activated * up_pre).astype(BF16)
        dup[k] = (d_hidden * activated).astype(BF16)
        dgate[k] = (d_hidden * up_pre * (sig + activated * (1.0 - sig))).astype(BF16)

    total_out, total_in = None, None
    for k in range(pieces):
        cut = slice(k * piece, (k + 1) * piece)
        out_part = mm(hid[k], down_ref[cut, :])
        in_part = mm_nt(dgate[k], gate_ref[:, cut]) + mm_nt(dup[k], up_ref[:, cut])
        total_out = out_part if k == 0 else total_out + out_part
        total_in = in_part if k == 0 else total_in + in_part
    for b in range(blocks):
        at = slice(b * capacity, (b + 1) * capacity)
        target = keep_ref if b < blocks // 2 else give_ref
        out_rows = (total_out[at].astype(BF16).astype(F32) * shares[b]).astype(BF16)
        target[b % (blocks // 2), 0] = mm_tn(chosen[b], out_rows).astype(BF16)
        in_rows = total_in[at].astype(BF16)
        target[b % (blocks // 2), 1] = mm_tn(chosen[b], in_rows).astype(BF16)

    if saved:
        parts = staged[2:]
        all_rows = jnp.concatenate([saved[0][...], rows[...]], axis=0)
        all_cots = jnp.concatenate([saved[1][...], cots[...]], axis=0)
        half = all_rows.shape[1] // 2
        for n, j in enumerate((3, 1, 2, 0)):
            first, second = parts[2 * n : 2 * n + 2]
            quarter = place ^ j
            both = lambda old, new: jnp.concatenate([old[quarter], new[quarter]], axis=0)
            for k, d_pre in enumerate((both(saved[3], dgate), both(saved[4], dup))):
                part = mm_tn(all_rows, d_pre).astype(BF16)
                first[k] = part[:half]
                second[k] = part[half:]
            part = mm_tn(both(saved[2], hid), all_cots).astype(BF16)
            first[2] = part[:, :half]
            second[2] = part[:, half:]


def finish_kernel(*refs):
    gate_ref, up_ref, down_ref = refs[6:]
    half = gate_ref.shape[0] // 2
    for k in (0, 1):
        mine, got, late = (ref[...].astype(F32) for ref in refs[3 * k : 3 * k + 3])
        total = (mine + got + late).astype(BF16)
        at = slice(k * half, (k + 1) * half)
        gate_ref[at] = total[0]
        up_ref[at] = total[1]
        down_ref[:, at] = total[2]


def vmem():
    return pl.BlockSpec(memory_space=pltpu.VMEM)


def run_pack(tokens, cotangent, codes):
    count, width = tokens.shape
    return pl.pallas_call(
        pack_kernel,
        in_specs=[vmem()] * 3,
        out_specs=vmem(),
        out_shape=jax.ShapeDtypeStruct((2 * count + CODE_ROWS, width), BF16),
        compiler_params=pltpu.CompilerParams(vmem_limit_bytes=4 * 1024 * 1024),
        name="pack",
    )(tokens, cotangent, codes.T)


def run_arm(parts, capacity, weights, piece, saved=()):
    blocks = len(parts)
    width, hidden_width = weights[0].shape
    count = (parts[0].shape[0] - CODE_ROWS) // 2
    rows = blocks * capacity
    pieces = hidden_width // piece
    one = (3, width // 2, piece)
    made = [(rows, width)] * 2 + [(pieces, rows, piece)] * 3
    outs = [(blocks // 2, 2, count, width)] * 2
    outs += [one] * 8 if saved else made
    ins = (*parts, *weights, *saved)
    return pl.pallas_call(
        functools.partial(arm_kernel, blocks, len(outs)),
        in_specs=[vmem()] * len(ins),
        out_specs=[vmem()] * len(outs),
        out_shape=[jax.ShapeDtypeStruct(shape, BF16) for shape in outs],
        scratch_shapes=[pltpu.VMEM(shape, BF16) for shape in made] if saved else [],
        compiler_params=pltpu.CompilerParams(vmem_limit_bytes=VMEM_BYTES),
        cost_estimate=pl.CostEstimate(
            flops=(24 if saved else 12) * rows * width * hidden_width,
            bytes_accessed=12 << 20,
            transcendentals=0,
        ),
        name="arm_late" if saved else "arm_early",
    )(*ins)


def run_finish(*parts):
    _, half, share = parts[0].shape
    width = 2 * half
    outs = [(width, share), (width, share), (share, width)]
    return pl.pallas_call(
        finish_kernel,
        in_specs=[vmem()] * 6,
        out_specs=[vmem()] * 3,
        out_shape=[jax.ShapeDtypeStruct(shape, BF16) for shape in outs],
        compiler_params=pltpu.CompilerParams(vmem_limit_bytes=8 * 1024 * 1024),
        name="finish",
    )(*parts)


def on_line(tokens, codes, cotangent, w_gate, w_up, w_down):
    token_count, width = tokens.shape
    arm_count = lax.axis_size("expert")
    capacity = 4 * token_count // arm_count
    w_gate, w_up, w_down = w_gate[0], w_up[0], w_down[0]
    hidden_width = w_gate.shape[1]
    chunk = hidden_width // lax.axis_size("dp")
    z = lax.axis_index("expert") // 2
    edge = (z == 0) | (z == 3)

    def along(pairs):
        return [(2 * s + c, 2 * d + c) for s, d in pairs for c in (0, 1)]

    far = along([(0, 3), (3, 0), (1, 2), (2, 1)])
    near = along([(0, 1), (1, 0), (2, 3), (3, 2)])
    skip = along([(0, 2), (2, 3), (3, 1), (1, 0)])
    skip_back = along([(2, 0), (3, 2), (1, 3), (0, 1)])
    core = [(e, e ^ 1) for e in range(8)]
    x_pair = [(i, i ^ 1) for i in range(4)]
    y_pair = [(i, i ^ 2) for i in range(4)]
    send = lambda value, pairs: lax.ppermute(value, "expert", pairs)
    send_dp = lambda value, pairs: lax.ppermute(value, "dp", pairs)

    own = run_pack(tokens, cotangent, codes)
    add = lambda a, b: a.astype(F32) + b.astype(F32)
    run = functools.partial(
        run_arm,
        capacity=capacity,
        weights=(w_gate, w_up, w_down),
        piece=chunk,
    )
    from_far = send(own, far)
    from_near = send(own, near)
    keep, give, *saved = run([own, from_near, send(own, core), send(from_near, core)])
    from_skip = send(jnp.where(edge, own, from_far), skip)
    from_skip, keep = lax.optimization_barrier((from_skip, keep))
    got = send(give, core)
    for_own = add(keep[0], got[0])
    for_near = add(keep[1], got[1]).astype(BF16)
    keep, give, d0, d1, x0, x1, y0, y1, k0, k1 = run(
        [from_far, from_skip, send(from_far, core), send(from_skip, core)], saved=saved
    )
    got = send(give, core)
    for_far = add(keep[0], got[0])
    for_skip = add(keep[1], got[1]).astype(BF16)
    from_x, from_y = send_dp(d0, x_pair), send_dp(d1, y_pair)
    for_near, x0, y1 = lax.optimization_barrier((for_near, x0, y1))
    last_x, last_y = send_dp(x0, x_pair), send_dp(y1, y_pair)
    from_skip = send(for_skip, skip_back)
    from_skip, from_x, from_y = lax.optimization_barrier((from_skip, from_x, from_y))
    from_near = send(for_near, near)
    for_far = for_far + jnp.where(edge, 0.0, from_skip.astype(F32))
    from_far = send(for_far.astype(BF16), far)
    y0, x1 = add(y0, from_x).astype(BF16), add(x1, from_y).astype(BF16)
    y0, x1 = send_dp(y0, y_pair), send_dp(x1, x_pair)
    result = for_own + from_near + from_far + jnp.where(edge, from_skip.astype(F32), 0.0)
    head_output, grad_tokens = result[0].astype(BF16), result[1].astype(BF16)
    grads = run_finish(k0, last_x, y0, k1, last_y, x1)
    grad_gate, grad_up, grad_down = (part[None] for part in grads)
    return (head_output, grad_tokens, grad_gate, grad_up, grad_down)


def solution(mesh):
    on_square_of_lines = mesh.shape["dp"] == 4 and mesh.shape["expert"] == 8
    return jax.shard_map(
        on_line if on_square_of_lines else on_device,
        mesh=mesh,
        in_specs=(
            P(("dp", "expert"), None),
            P(("dp", "expert"), None),
            P(("dp", "expert"), None),
            P("expert", None, None),
            P("expert", None, None),
            P("expert", None, None),
        ),
        out_specs=(
            P(("dp", "expert"), None),
            P(("dp", "expert"), None),
            P("expert", None, "dp"),
            P("expert", None, "dp"),
            P("expert", "dp", None),
        ),
        check_vma=False,
    )
```

```python
import functools

import jax
import jax.numpy as jnp
from jax import lax
from jax.experimental import pallas as pl
from jax.experimental.pallas import tpu as pltpu
from jax.sharding import PartitionSpec as P

fact_share = 0.7
counter_share = 0.3

F32 = jnp.float32
BF16 = jnp.bfloat16
CODE_ROWS = 16
VMEM_BYTES = 16 * 1024 * 1024

def rounded(value):
    return lax.optimization_barrier(value.astype(jnp.bfloat16)).astype(jnp.float32)


def silu_parts(gate_pre):
    sigmoid_gate = jax.nn.sigmoid(gate_pre)
    return (gate_pre * sigmoid_gate, sigmoid_gate * (1.0 + gate_pre * (1.0 - sigmoid_gate)))


def arm_forward(rows_in, gate_w, up_w):
    gate_pre = jnp.einsum("arc,ach->arh", rows_in, gate_w, preferred_element_type=jnp.float32)
    up_pre = jnp.einsum("arc,ach->arh", rows_in, up_w, preferred_element_type=jnp.float32)
    activated, silu_slope = silu_parts(gate_pre)
    hidden = (activated * up_pre).astype(jnp.bfloat16)
    return (up_pre, activated, silu_slope, hidden)


def arm_backward(up_pre, activated, silu_slope, cot_in, down_w):
    d_hidden = jnp.einsum("arc,ahc->arh", cot_in, down_w, preferred_element_type=jnp.float32)
    d_up = (d_hidden * activated).astype(jnp.bfloat16)
    d_gate = (d_hidden * up_pre * silu_slope).astype(jnp.bfloat16)
    return (d_gate, d_up)


def on_device(tokens, codes, cotangent, w_gate, w_up, w_down):
    token_count, feature_width = tokens.shape
    local_arms = w_gate.shape[0]
    arm_count = local_arms * lax.axis_size("expert")
    capacity = 4 * token_count // arm_count
    flat_codes = codes.reshape(-1)
    arm_ids = jnp.arange(arm_count, dtype=jnp.int32)
    onehot = (flat_codes[:, None] == arm_ids[None, :]).astype(jnp.int32)
    earlier = jnp.cumsum(onehot, axis=0) - onehot
    destination = flat_codes * capacity + jnp.sum(earlier * onehot, axis=1)
    shares = jnp.tile(jnp.array([fact_share, counter_share], jnp.float32), token_count)
    token_rows = jnp.repeat(tokens, 2, axis=0)
    cot_rows = (jnp.repeat(cotangent.astype(jnp.float32), 2, axis=0) * shares[:, None]).astype(
        jnp.bfloat16
    )
    blank_rows = jnp.zeros((arm_count * capacity, feature_width), jnp.bfloat16)
    send_tokens = (
        blank_rows.at[destination].set(token_rows).reshape(arm_count, capacity, feature_width)
    )
    send_cot = blank_rows.at[destination].set(cot_rows).reshape(arm_count, capacity, feature_width)
    arm_tokens, arm_cot = (
        lax.all_to_all(send_tokens, "expert", split_axis=0, concat_axis=1, tiled=True),
        lax.all_to_all(send_cot, "expert", split_axis=0, concat_axis=1, tiled=True),
    )
    up_pre, activated, silu_slope, hidden = arm_forward(arm_tokens, w_gate, w_up)
    out_rows = jnp.einsum(
        "arh,ahc->arc", hidden, w_down, preferred_element_type=jnp.float32
    ).astype(jnp.bfloat16)
    d_gate, d_up = arm_backward(up_pre, activated, silu_slope, arm_cot, w_down)
    input_rows = (
        jnp.einsum("arh,ach->arc", d_gate, w_gate, preferred_element_type=jnp.float32)
        + jnp.einsum("arh,ach->arc", d_up, w_up, preferred_element_type=jnp.float32)
    ).astype(jnp.bfloat16)
    back_out, back_input = (
        lax.all_to_all(out_rows, "expert", split_axis=1, concat_axis=0, tiled=True),
        lax.all_to_all(input_rows, "expert", split_axis=1, concat_axis=0, tiled=True),
    )
    back_out = back_out.reshape(arm_count * capacity, feature_width)[destination]
    back_out = back_out.reshape(token_count, 2, feature_width).astype(jnp.float32)
    back_input = back_input.reshape(arm_count * capacity, feature_width)[destination]
    back_input = back_input.reshape(token_count, 2, feature_width).astype(jnp.float32)
    head_output = (fact_share * back_out[:, 0] + counter_share * back_out[:, 1]).astype(
        jnp.bfloat16
    )
    grad_tokens = (back_input[:, 0] + back_input[:, 1]).astype(jnp.bfloat16)
    all_tokens, all_cot = (
        lax.all_gather(arm_tokens, "dp", axis=1, tiled=True),
        lax.all_gather(arm_cot, "dp", axis=1, tiled=True),
    )
    group_count = lax.axis_size("dp")
    hidden_width = w_gate.shape[2]
    quarter = hidden_width // group_count
    first_unit = lax.axis_index("dp") * quarter
    gate_share = lax.dynamic_slice_in_dim(w_gate, first_unit, quarter, 2)
    up_share = lax.dynamic_slice_in_dim(w_up, first_unit, quarter, 2)
    down_share = lax.dynamic_slice_in_dim(w_down, first_unit, quarter, 1)
    row_count = arm_tokens.shape[1]
    total_gate = jnp.zeros((local_arms, feature_width, quarter), jnp.float32)
    total_up = jnp.zeros((local_arms, feature_width, quarter), jnp.float32)
    total_down = jnp.zeros((local_arms, quarter, feature_width), jnp.float32)
    for group_index in range(group_count):
        some_tokens = all_tokens[:, group_index * row_count : (group_index + 1) * row_count]
        some_cot = all_cot[:, group_index * row_count : (group_index + 1) * row_count]
        piece_up, piece_act, piece_slope, piece_hidden = arm_forward(
            some_tokens, gate_share, up_share
        )
        piece_dgate, piece_dup = arm_backward(
            piece_up, piece_act, piece_slope, some_cot, down_share
        )
        total_gate = total_gate + rounded(
            jnp.einsum("arc,arh->ach", some_tokens, piece_dgate, preferred_element_type=jnp.float32)
        )
        total_up = total_up + rounded(
            jnp.einsum("arc,arh->ach", some_tokens, piece_dup, preferred_element_type=jnp.float32)
        )
        total_down = total_down + rounded(
            jnp.einsum("arh,arc->ahc", piece_hidden, some_cot, preferred_element_type=jnp.float32)
        )
    grad_gate = total_gate.astype(jnp.bfloat16)
    grad_up = total_up.astype(jnp.bfloat16)
    grad_down = total_down.astype(jnp.bfloat16)
    return (head_output, grad_tokens, grad_gate, grad_up, grad_down)


def mm(left, right):
    return jnp.dot(left, right, preferred_element_type=F32)


def mm_nt(left, right):
    return lax.dot_general(left, right, (((1,), (1,)), ((), ())), preferred_element_type=F32)


def mm_tn(left, right):
    return lax.dot_general(left, right, (((0,), (0,)), ((), ())), preferred_element_type=F32)


def selections(code_tiles, arm, capacity):
    count = code_tiles[0].shape[1]
    named = [(tile.astype(F32) == arm).astype(F32) for tile in code_tiles]
    before = lax.broadcasted_iota(jnp.int32, (count, count), 0)
    after = lax.broadcasted_iota(jnp.int32, (count, count), 1)
    ranks = mm(jnp.concatenate(named, axis=0).astype(BF16), (before < after).astype(BF16))
    slot = lax.broadcasted_iota(jnp.int32, (capacity, count), 0).astype(F32)
    chosen, shares = [], []
    for b, hit in enumerate(named):
        rank = ranks[b * CODE_ROWS : b * CODE_ROWS + 1] + ranks[b * CODE_ROWS + 1 : b * CODE_ROWS + 2]
        here = jnp.where(slot == rank, hit[0:1] + hit[1:2], 0.0)
        share = fact_share * hit[0:1] + counter_share * hit[1:2]
        chosen.append(here.astype(BF16))
        shares.append(jnp.sum(here * share, axis=1, keepdims=True))
    return chosen, shares


def pack_kernel(tokens_ref, cot_ref, codes_ref, out_ref):
    count = tokens_ref.shape[0]
    out_ref[0:count] = tokens_ref[...]
    out_ref[count : 2 * count] = cot_ref[...]
    out_ref[2 * count : 2 * count + CODE_ROWS] = jnp.zeros((CODE_ROWS, out_ref.shape[1]), BF16)
    rows = lax.broadcasted_iota(jnp.int32, (CODE_ROWS, count), 0)
    codes = codes_ref[...].astype(F32)
    both = jnp.where(rows == 0, codes[0:1], jnp.where(rows == 1, codes[1:2], 0.0))
    out_ref[2 * count : 2 * count + CODE_ROWS, 0:count] = both.astype(BF16)


def arm_kernel(blocks, outs_count, *refs):
    held, refs = refs[:blocks], refs[blocks:]
    (gate_ref, up_ref, down_ref), refs = refs[:3], refs[3:]
    saved, refs = (refs[:5], refs[5:]) if outs_count == 10 else ((), refs)
    staged, made = refs[:outs_count], refs[outs_count:]
    keep_ref, give_ref = staged[:2]
    rows, cots, hid, dgate, dup = made if saved else staged[2:]
    capacity, count = rows.shape[0] // blocks, keep_ref.shape[2]
    pieces = hid.shape[0]
    arm, place = lax.axis_index("expert"), lax.axis_index("dp")

    tiles = [ref[2 * count : 2 * count + CODE_ROWS, 0:count] for ref in held]
    chosen, shares = selections(tiles, arm.astype(F32), capacity)
    for b in range(blocks):
        at = slice(b * capacity, (b + 1) * capacity)
        rows[at] = mm(chosen[b], held[b][0:count]).astype(BF16)
        picked = mm(chosen[b], held[b][count : 2 * count])
        cots[at] = (picked * shares[b]).astype(BF16)

    for k in range(pieces):
        piece = hid.shape[2]
        cut = slice(k * piece, (k + 1) * piece)
        gate_pre = mm(rows[...], gate_ref[:, cut])
        up_pre = mm(rows[...], up_ref[:, cut])
        d_hidden = mm_nt(cots[...], down_ref[cut, :])
        sig = 0.5 * jnp.tanh(0.5 * gate_pre) + 0.5
        activated = gate_pre * sig
        hid[k] = (activated * up_pre).astype(BF16)
        dup[k] = (d_hidden * activated).astype(BF16)
        dgate[k] = (d_hidden * up_pre * (sig + activated * (1.0 - sig))).astype(BF16)

    total_out, total_in = None, None
    for k in range(pieces):
        cut = slice(k * piece, (k + 1) * piece)
        out_part = mm(hid[k], down_ref[cut, :])
        in_part = mm_nt(dgate[k], gate_ref[:, cut]) + mm_nt(dup[k], up_ref[:, cut])
        total_out = out_part if k == 0 else total_out + out_part
        total_in = in_part if k == 0 else total_in + in_part
    for b in range(blocks):
        at = slice(b * capacity, (b + 1) * capacity)
        target = keep_ref if b < blocks // 2 else give_ref
        out_rows = (total_out[at].astype(BF16).astype(F32) * shares[b]).astype(BF16)
        target[b % (blocks // 2), 0] = mm_tn(chosen[b], out_rows).astype(BF16)
        in_rows = total_in[at].astype(BF16)
        target[b % (blocks // 2), 1] = mm_tn(chosen[b], in_rows).astype(BF16)

    if saved:
        parts = staged[2:]
        all_rows = jnp.concatenate([saved[0][...], rows[...]], axis=0)
        all_cots = jnp.concatenate([saved[1][...], cots[...]], axis=0)
        half = all_rows.shape[1] // 2
        for n, j in enumerate((3, 1, 2, 0)):
            first, second = parts[2 * n : 2 * n + 2]
            quarter = place ^ j
            both = lambda old, new: jnp.concatenate([old[quarter], new[quarter]], axis=0)
            d_pre = jnp.concatenate([both(saved[3], dgate), both(saved[4], dup)], axis=1)
            part = mm_tn(all_rows, d_pre).astype(BF16)
            for k in (0, 1):
                at = slice(k * dgate.shape[2], (k + 1) * dgate.shape[2])
                first[k] = part[:half, at]
                second[k] = part[half:, at]
            part = mm_tn(both(saved[2], hid), all_cots).astype(BF16)
            first[2] = part[:, :half]
            second[2] = part[:, half:]


def finish_kernel(*refs):
    gate_ref, up_ref, down_ref = refs[6:]
    half = gate_ref.shape[0] // 2
    for k in (0, 1):
        mine, got, late = (ref[...].astype(F32) for ref in refs[3 * k : 3 * k + 3])
        total = (mine + got + late).astype(BF16)
        at = slice(k * half, (k + 1) * half)
        gate_ref[at] = total[0]
        up_ref[at] = total[1]
        down_ref[:, at] = total[2]


def vmem():
    return pl.BlockSpec(memory_space=pltpu.VMEM)


def run_pack(tokens, cotangent, codes):
    count, width = tokens.shape
    return pl.pallas_call(
        pack_kernel,
        in_specs=[vmem()] * 3,
        out_specs=vmem(),
        out_shape=jax.ShapeDtypeStruct((2 * count + CODE_ROWS, width), BF16),
        compiler_params=pltpu.CompilerParams(vmem_limit_bytes=4 * 1024 * 1024),
        name="pack",
    )(tokens, cotangent, codes.T)


def run_arm(parts, capacity, weights, piece, saved=()):
    blocks = len(parts)
    width, hidden_width = weights[0].shape
    count = (parts[0].shape[0] - CODE_ROWS) // 2
    rows = blocks * capacity
    pieces = hidden_width // piece
    one = (3, width // 2, piece)
    made = [(rows, width)] * 2 + [(pieces, rows, piece)] * 3
    outs = [(blocks // 2, 2, count, width)] * 2
    outs += [one] * 8 if saved else made
    ins = (*parts, *weights, *saved)
    return pl.pallas_call(
        functools.partial(arm_kernel, blocks, len(outs)),
        in_specs=[vmem()] * len(ins),
        out_specs=[vmem()] * len(outs),
        out_shape=[jax.ShapeDtypeStruct(shape, BF16) for shape in outs],
        scratch_shapes=[pltpu.VMEM(shape, BF16) for shape in made] if saved else [],
        compiler_params=pltpu.CompilerParams(vmem_limit_bytes=VMEM_BYTES),
        cost_estimate=pl.CostEstimate(
            flops=(24 if saved else 12) * rows * width * hidden_width,
            bytes_accessed=12 << 20,
            transcendentals=0,
        ),
        name="arm_late" if saved else "arm_early",
    )(*ins)


def run_finish(*parts):
    _, half, share = parts[0].shape
    width = 2 * half
    outs = [(width, share), (width, share), (share, width)]
    return pl.pallas_call(
        finish_kernel,
        in_specs=[vmem()] * 6,
        out_specs=[vmem()] * 3,
        out_shape=[jax.ShapeDtypeStruct(shape, BF16) for shape in outs],
        compiler_params=pltpu.CompilerParams(vmem_limit_bytes=8 * 1024 * 1024),
        name="finish",
    )(*parts)


def on_line(tokens, codes, cotangent, w_gate, w_up, w_down):
    token_count, width = tokens.shape
    arm_count = lax.axis_size("expert")
    capacity = 4 * token_count // arm_count
    w_gate, w_up, w_down = w_gate[0], w_up[0], w_down[0]
    hidden_width = w_gate.shape[1]
    chunk = hidden_width // lax.axis_size("dp")
    z = lax.axis_index("expert") // 2
    edge = (z == 0) | (z == 3)

    def along(pairs):
        return [(2 * s + c, 2 * d + c) for s, d in pairs for c in (0, 1)]

    far = along([(0, 3), (3, 0), (1, 2), (2, 1)])
    near = along([(0, 1), (1, 0), (2, 3), (3, 2)])
    skip = along([(0, 2), (2, 3), (3, 1), (1, 0)])
    skip_back = along([(2, 0), (3, 2), (1, 3), (0, 1)])
    core = [(e, e ^ 1) for e in range(8)]
    x_pair = [(i, i ^ 1) for i in range(4)]
    y_pair = [(i, i ^ 2) for i in range(4)]
    send = lambda value, pairs: lax.ppermute(value, "expert", pairs)
    send_dp = lambda value, pairs: lax.ppermute(value, "dp", pairs)

    own = run_pack(tokens, cotangent, codes)
    add = lambda a, b: a.astype(F32) + b.astype(F32)
    run = functools.partial(
        run_arm,
        capacity=capacity,
        weights=(w_gate, w_up, w_down),
        piece=chunk,
    )
    from_far = send(own, far)
    from_near = send(own, near)
    keep, give, *saved = run([own, from_near, send(own, core), send(from_near, core)])
    from_skip = send(jnp.where(edge, own, from_far), skip)
    from_skip, keep = lax.optimization_barrier((from_skip, keep))
    got = send(give, core)
    for_own = add(keep[0], got[0])
    for_near = add(keep[1], got[1]).astype(BF16)
    keep, give, d0, d1, x0, x1, y0, y1, k0, k1 = run(
        [from_far, from_skip, send(from_far, core), send(from_skip, core)], saved=saved
    )
    got = send(give, core)
    for_far = add(keep[0], got[0])
    for_skip = add(keep[1], got[1]).astype(BF16)
    from_x, from_y = send_dp(d0, x_pair), send_dp(d1, y_pair)
    last_x, last_y = send_dp(x0, x_pair), send_dp(y1, y_pair)
    from_skip = send(for_skip, skip_back)
    from_skip, from_x, from_y = lax.optimization_barrier((from_skip, from_x, from_y))
    from_near = send(for_near, near)
    for_far = for_far + jnp.where(edge, 0.0, from_skip.astype(F32))
    from_far = send(for_far.astype(BF16), far)
    y0, x1 = add(y0, from_x).astype(BF16), add(x1, from_y).astype(BF16)
    y0, x1 = send_dp(y0, y_pair), send_dp(x1, x_pair)
    from_far, from_near = lax.optimization_barrier((from_far, from_near))
    result = for_own + from_near + from_far + jnp.where(edge, from_skip.astype(F32), 0.0)
    head_output, grad_tokens = result[0].astype(BF16), result[1].astype(BF16)
    grads = run_finish(k0, last_x, y0, k1, last_y, x1)
    grad_gate, grad_up, grad_down = (part[None] for part in grads)
    return (head_output, grad_tokens, grad_gate, grad_up, grad_down)


def solution(mesh):
    on_square_of_lines = mesh.shape["dp"] == 4 and mesh.shape["expert"] == 8
    return jax.shard_map(
        on_line if on_square_of_lines else on_device,
        mesh=mesh,
        in_specs=(
            P(("dp", "expert"), None),
            P(("dp", "expert"), None),
            P(("dp", "expert"), None),
            P("expert", None, None),
            P("expert", None, None),
            P("expert", None, None),
        ),
        out_specs=(
            P(("dp", "expert"), None),
            P(("dp", "expert"), None),
            P("expert", None, "dp"),
            P("expert", None, "dp"),
            P("expert", "dp", None),
        ),
        check_vma=False,
    )
```

```python
import functools

import jax
import jax.numpy as jnp
from jax import lax
from jax.experimental import pallas as pl
from jax.experimental.pallas import tpu as pltpu
from jax.sharding import PartitionSpec as P

fact_share = 0.7
counter_share = 0.3

F32 = jnp.float32
BF16 = jnp.bfloat16
CODE_ROWS = 16
VMEM_BYTES = 24 * 1024 * 1024

def rounded(value):
    return lax.optimization_barrier(value.astype(jnp.bfloat16)).astype(jnp.float32)


def silu_parts(gate_pre):
    sigmoid_gate = jax.nn.sigmoid(gate_pre)
    return (gate_pre * sigmoid_gate, sigmoid_gate * (1.0 + gate_pre * (1.0 - sigmoid_gate)))


def arm_forward(rows_in, gate_w, up_w):
    gate_pre = jnp.einsum("arc,ach->arh", rows_in, gate_w, preferred_element_type=jnp.float32)
    up_pre = jnp.einsum("arc,ach->arh", rows_in, up_w, preferred_element_type=jnp.float32)
    activated, silu_slope = silu_parts(gate_pre)
    hidden = (activated * up_pre).astype(jnp.bfloat16)
    return (up_pre, activated, silu_slope, hidden)


def arm_backward(up_pre, activated, silu_slope, cot_in, down_w):
    d_hidden = jnp.einsum("arc,ahc->arh", cot_in, down_w, preferred_element_type=jnp.float32)
    d_up = (d_hidden * activated).astype(jnp.bfloat16)
    d_gate = (d_hidden * up_pre * silu_slope).astype(jnp.bfloat16)
    return (d_gate, d_up)


def on_device(tokens, codes, cotangent, w_gate, w_up, w_down):
    token_count, feature_width = tokens.shape
    local_arms = w_gate.shape[0]
    arm_count = local_arms * lax.axis_size("expert")
    capacity = 4 * token_count // arm_count
    flat_codes = codes.reshape(-1)
    arm_ids = jnp.arange(arm_count, dtype=jnp.int32)
    onehot = (flat_codes[:, None] == arm_ids[None, :]).astype(jnp.int32)
    earlier = jnp.cumsum(onehot, axis=0) - onehot
    destination = flat_codes * capacity + jnp.sum(earlier * onehot, axis=1)
    shares = jnp.tile(jnp.array([fact_share, counter_share], jnp.float32), token_count)
    token_rows = jnp.repeat(tokens, 2, axis=0)
    cot_rows = (jnp.repeat(cotangent.astype(jnp.float32), 2, axis=0) * shares[:, None]).astype(
        jnp.bfloat16
    )
    blank_rows = jnp.zeros((arm_count * capacity, feature_width), jnp.bfloat16)
    send_tokens = (
        blank_rows.at[destination].set(token_rows).reshape(arm_count, capacity, feature_width)
    )
    send_cot = blank_rows.at[destination].set(cot_rows).reshape(arm_count, capacity, feature_width)
    arm_tokens, arm_cot = (
        lax.all_to_all(send_tokens, "expert", split_axis=0, concat_axis=1, tiled=True),
        lax.all_to_all(send_cot, "expert", split_axis=0, concat_axis=1, tiled=True),
    )
    up_pre, activated, silu_slope, hidden = arm_forward(arm_tokens, w_gate, w_up)
    out_rows = jnp.einsum(
        "arh,ahc->arc", hidden, w_down, preferred_element_type=jnp.float32
    ).astype(jnp.bfloat16)
    d_gate, d_up = arm_backward(up_pre, activated, silu_slope, arm_cot, w_down)
    input_rows = (
        jnp.einsum("arh,ach->arc", d_gate, w_gate, preferred_element_type=jnp.float32)
        + jnp.einsum("arh,ach->arc", d_up, w_up, preferred_element_type=jnp.float32)
    ).astype(jnp.bfloat16)
    back_out, back_input = (
        lax.all_to_all(out_rows, "expert", split_axis=1, concat_axis=0, tiled=True),
        lax.all_to_all(input_rows, "expert", split_axis=1, concat_axis=0, tiled=True),
    )
    back_out = back_out.reshape(arm_count * capacity, feature_width)[destination]
    back_out = back_out.reshape(token_count, 2, feature_width).astype(jnp.float32)
    back_input = back_input.reshape(arm_count * capacity, feature_width)[destination]
    back_input = back_input.reshape(token_count, 2, feature_width).astype(jnp.float32)
    head_output = (fact_share * back_out[:, 0] + counter_share * back_out[:, 1]).astype(
        jnp.bfloat16
    )
    grad_tokens = (back_input[:, 0] + back_input[:, 1]).astype(jnp.bfloat16)
    all_tokens, all_cot = (
        lax.all_gather(arm_tokens, "dp", axis=1, tiled=True),
        lax.all_gather(arm_cot, "dp", axis=1, tiled=True),
    )
    group_count = lax.axis_size("dp")
    hidden_width = w_gate.shape[2]
    quarter = hidden_width // group_count
    first_unit = lax.axis_index("dp") * quarter
    gate_share = lax.dynamic_slice_in_dim(w_gate, first_unit, quarter, 2)
    up_share = lax.dynamic_slice_in_dim(w_up, first_unit, quarter, 2)
    down_share = lax.dynamic_slice_in_dim(w_down, first_unit, quarter, 1)
    row_count = arm_tokens.shape[1]
    total_gate = jnp.zeros((local_arms, feature_width, quarter), jnp.float32)
    total_up = jnp.zeros((local_arms, feature_width, quarter), jnp.float32)
    total_down = jnp.zeros((local_arms, quarter, feature_width), jnp.float32)
    for group_index in range(group_count):
        some_tokens = all_tokens[:, group_index * row_count : (group_index + 1) * row_count]
        some_cot = all_cot[:, group_index * row_count : (group_index + 1) * row_count]
        piece_up, piece_act, piece_slope, piece_hidden = arm_forward(
            some_tokens, gate_share, up_share
        )
        piece_dgate, piece_dup = arm_backward(
            piece_up, piece_act, piece_slope, some_cot, down_share
        )
        total_gate = total_gate + rounded(
            jnp.einsum("arc,arh->ach", some_tokens, piece_dgate, preferred_element_type=jnp.float32)
        )
        total_up = total_up + rounded(
            jnp.einsum("arc,arh->ach", some_tokens, piece_dup, preferred_element_type=jnp.float32)
        )
        total_down = total_down + rounded(
            jnp.einsum("arh,arc->ahc", piece_hidden, some_cot, preferred_element_type=jnp.float32)
        )
    grad_gate = total_gate.astype(jnp.bfloat16)
    grad_up = total_up.astype(jnp.bfloat16)
    grad_down = total_down.astype(jnp.bfloat16)
    return (head_output, grad_tokens, grad_gate, grad_up, grad_down)


def mm(left, right):
    return jnp.dot(left, right, preferred_element_type=F32)


def mm_nt(left, right):
    return lax.dot_general(left, right, (((1,), (1,)), ((), ())), preferred_element_type=F32)


def mm_tn(left, right):
    return lax.dot_general(left, right, (((0,), (0,)), ((), ())), preferred_element_type=F32)


def selections(code_tiles, arm, capacity):
    count = code_tiles[0].shape[1]
    named = [(tile.astype(F32) == arm).astype(F32) for tile in code_tiles]
    before = lax.broadcasted_iota(jnp.int32, (count, count), 0)
    after = lax.broadcasted_iota(jnp.int32, (count, count), 1)
    ranks = mm(jnp.concatenate(named, axis=0).astype(BF16), (before < after).astype(BF16))
    slot = lax.broadcasted_iota(jnp.int32, (capacity, count), 0).astype(F32)
    chosen, shares = [], []
    for b, hit in enumerate(named):
        rank = ranks[b * CODE_ROWS : b * CODE_ROWS + 1] + ranks[b * CODE_ROWS + 1 : b * CODE_ROWS + 2]
        here = jnp.where(slot == rank, hit[0:1] + hit[1:2], 0.0)
        share = fact_share * hit[0:1] + counter_share * hit[1:2]
        chosen.append(here.astype(BF16))
        shares.append(jnp.sum(here * share, axis=1, keepdims=True))
    return chosen, shares


def pack_kernel(tokens_ref, cot_ref, codes_ref, out_ref):
    count = tokens_ref.shape[0]
    out_ref[0:count] = tokens_ref[...]
    out_ref[count : 2 * count] = cot_ref[...]
    out_ref[2 * count : 2 * count + CODE_ROWS] = jnp.zeros((CODE_ROWS, out_ref.shape[1]), BF16)
    rows = lax.broadcasted_iota(jnp.int32, (CODE_ROWS, count), 0)
    codes = codes_ref[...].astype(F32)
    both = jnp.where(rows == 0, codes[0:1], jnp.where(rows == 1, codes[1:2], 0.0))
    out_ref[2 * count : 2 * count + CODE_ROWS, 0:count] = both.astype(BF16)


def arm_kernel(blocks, outs_count, *refs):
    held, refs = refs[:blocks], refs[blocks:]
    (gate_ref, up_ref, down_ref), refs = refs[:3], refs[3:]
    saved, refs = (refs[:5], refs[5:]) if outs_count == 10 else ((), refs)
    staged, made = refs[:outs_count], refs[outs_count:]
    keep_ref, give_ref = staged[:2]
    rows, cots, hid, dgate, dup = made if saved else staged[2:]
    capacity, count = rows.shape[0] // blocks, keep_ref.shape[2]
    pieces = hid.shape[0]
    arm, place = lax.axis_index("expert"), lax.axis_index("dp")

    tiles = [ref[2 * count : 2 * count + CODE_ROWS, 0:count] for ref in held]
    chosen, shares = selections(tiles, arm.astype(F32), capacity)
    for b in range(blocks):
        at = slice(b * capacity, (b + 1) * capacity)
        rows[at] = mm(chosen[b], held[b][0:count]).astype(BF16)
        picked = mm(chosen[b], held[b][count : 2 * count])
        cots[at] = (picked * shares[b]).astype(BF16)

    for k in range(pieces):
        piece = hid.shape[2]
        cut = slice(k * piece, (k + 1) * piece)
        gate_pre = mm(rows[...], gate_ref[:, cut])
        up_pre = mm(rows[...], up_ref[:, cut])
        d_hidden = mm_nt(cots[...], down_ref[cut, :])
        sig = 0.5 * jnp.tanh(0.5 * gate_pre) + 0.5
        activated = gate_pre * sig
        hid[k] = (activated * up_pre).astype(BF16)
        dup[k] = (d_hidden * activated).astype(BF16)
        dgate[k] = (d_hidden * up_pre * (sig + activated * (1.0 - sig))).astype(BF16)

    total_out, total_in = None, None
    for k in range(pieces):
        cut = slice(k * piece, (k + 1) * piece)
        out_part = mm(hid[k], down_ref[cut, :])
        in_part = mm_nt(dgate[k], gate_ref[:, cut]) + mm_nt(dup[k], up_ref[:, cut])
        total_out = out_part if k == 0 else total_out + out_part
        total_in = in_part if k == 0 else total_in + in_part
    for b in range(blocks):
        at = slice(b * capacity, (b + 1) * capacity)
        target = keep_ref if b < blocks // 2 else give_ref
        out_rows = (total_out[at].astype(BF16).astype(F32) * shares[b]).astype(BF16)
        target[b % (blocks // 2), 0] = mm_tn(chosen[b], out_rows).astype(BF16)
        in_rows = total_in[at].astype(BF16)
        target[b % (blocks // 2), 1] = mm_tn(chosen[b], in_rows).astype(BF16)

    if saved:
        parts = staged[2:]
        all_rows = jnp.concatenate([saved[0][...], rows[...]], axis=0)
        all_cots = jnp.concatenate([saved[1][...], cots[...]], axis=0)
        half = all_rows.shape[1] // 2
        for n, j in enumerate((3, 1, 2, 0)):
            first, second = parts[2 * n : 2 * n + 2]
            quarter = place ^ j
            both = lambda old, new: jnp.concatenate([old[quarter], new[quarter]], axis=0)
            d_pre = jnp.concatenate([both(saved[3], dgate), both(saved[4], dup)], axis=1)
            part = mm_tn(all_rows, d_pre).astype(BF16)
            for k in (0, 1):
                at = slice(k * dgate.shape[2], (k + 1) * dgate.shape[2])
                first[k] = part[:half, at]
                second[k] = part[half:, at]
            part = mm_tn(both(saved[2], hid), all_cots).astype(BF16)
            first[2] = part[:, :half]
            second[2] = part[:, half:]


def finish_kernel(*refs):
    gate_ref, up_ref, down_ref = refs[6:]
    half = gate_ref.shape[0] // 2
    for k in (0, 1):
        mine, got, late = (ref[...].astype(F32) for ref in refs[3 * k : 3 * k + 3])
        total = (mine + got + late).astype(BF16)
        at = slice(k * half, (k + 1) * half)
        gate_ref[at] = total[0]
        up_ref[at] = total[1]
        down_ref[:, at] = total[2]


def vmem():
    return pl.BlockSpec(memory_space=pltpu.VMEM)


def run_pack(tokens, cotangent, codes):
    count, width = tokens.shape
    return pl.pallas_call(
        pack_kernel,
        in_specs=[vmem()] * 3,
        out_specs=vmem(),
        out_shape=jax.ShapeDtypeStruct((2 * count + CODE_ROWS, width), BF16),
        compiler_params=pltpu.CompilerParams(vmem_limit_bytes=4 * 1024 * 1024),
        name="pack",
    )(tokens, cotangent, codes.T)


def run_arm(parts, capacity, weights, piece, saved=()):
    blocks = len(parts)
    width, hidden_width = weights[0].shape
    count = (parts[0].shape[0] - CODE_ROWS) // 2
    rows = blocks * capacity
    pieces = hidden_width // piece
    one = (3, width // 2, piece)
    made = [(rows, width)] * 2 + [(pieces, rows, piece)] * 3
    outs = [(blocks // 2, 2, count, width)] * 2
    outs += [one] * 8 if saved else made
    ins = (*parts, *weights, *saved)
    return pl.pallas_call(
        functools.partial(arm_kernel, blocks, len(outs)),
        in_specs=[vmem()] * len(ins),
        out_specs=[vmem()] * len(outs),
        out_shape=[jax.ShapeDtypeStruct(shape, BF16) for shape in outs],
        scratch_shapes=[pltpu.VMEM(shape, BF16) for shape in made] if saved else [],
        compiler_params=pltpu.CompilerParams(vmem_limit_bytes=VMEM_BYTES),
        cost_estimate=pl.CostEstimate(
            flops=(24 if saved else 12) * rows * width * hidden_width,
            bytes_accessed=12 << 20,
            transcendentals=0,
        ),
        name="arm_late" if saved else "arm_early",
    )(*ins)


def run_finish(*parts):
    _, half, share = parts[0].shape
    width = 2 * half
    outs = [(width, share), (width, share), (share, width)]
    return pl.pallas_call(
        finish_kernel,
        in_specs=[vmem()] * 6,
        out_specs=[vmem()] * 3,
        out_shape=[jax.ShapeDtypeStruct(shape, BF16) for shape in outs],
        compiler_params=pltpu.CompilerParams(vmem_limit_bytes=8 * 1024 * 1024),
        name="finish",
    )(*parts)


def on_line(tokens, codes, cotangent, w_gate, w_up, w_down):
    token_count, width = tokens.shape
    arm_count = lax.axis_size("expert")
    capacity = 4 * token_count // arm_count
    w_gate, w_up, w_down = w_gate[0], w_up[0], w_down[0]
    hidden_width = w_gate.shape[1]
    chunk = hidden_width // lax.axis_size("dp")
    z = lax.axis_index("expert") // 2
    edge = (z == 0) | (z == 3)

    def along(pairs):
        return [(2 * s + c, 2 * d + c) for s, d in pairs for c in (0, 1)]

    far = along([(0, 3), (3, 0), (1, 2), (2, 1)])
    near = along([(0, 1), (1, 0), (2, 3), (3, 2)])
    skip = along([(0, 2), (2, 3), (3, 1), (1, 0)])
    skip_back = along([(2, 0), (3, 2), (1, 3), (0, 1)])
    core = [(e, e ^ 1) for e in range(8)]
    x_pair = [(i, i ^ 1) for i in range(4)]
    y_pair = [(i, i ^ 2) for i in range(4)]
    send = lambda value, pairs: lax.ppermute(value, "expert", pairs)
    send_dp = lambda value, pairs: lax.ppermute(value, "dp", pairs)

    own = run_pack(tokens, cotangent, codes)
    add = lambda a, b: a.astype(F32) + b.astype(F32)
    run = functools.partial(
        run_arm,
        capacity=capacity,
        weights=(w_gate, w_up, w_down),
        piece=chunk,
    )
    from_far = send(own, far)
    from_near = send(own, near)
    keep, give, *saved = run([own, from_near, send(own, core), send(from_near, core)])
    from_skip = send(jnp.where(edge, own, from_far), skip)
    from_skip, keep = lax.optimization_barrier((from_skip, keep))
    got = send(give, core)
    for_own = add(keep[0], got[0])
    for_near = add(keep[1], got[1]).astype(BF16)
    keep, give, d0, d1, x0, x1, y0, y1, k0, k1 = run(
        [from_far, from_skip, send(from_far, core), send(from_skip, core)], saved=saved
    )
    got = send(give, core)
    for_far = add(keep[0], got[0])
    for_skip = add(keep[1], got[1]).astype(BF16)
    from_x, from_y = send_dp(d0, x_pair), send_dp(d1, y_pair)
    last_x, last_y = send_dp(x0, x_pair), send_dp(y1, y_pair)
    from_skip = send(for_skip, skip_back)
    from_skip, from_x, from_y = lax.optimization_barrier((from_skip, from_x, from_y))
    from_near = send(for_near, near)
    for_far = for_far + jnp.where(edge, 0.0, from_skip.astype(F32))
    from_far = send(for_far.astype(BF16), far)
    y0, x1 = add(y0, from_x).astype(BF16), add(x1, from_y).astype(BF16)
    y0, x1 = send_dp(y0, y_pair), send_dp(x1, x_pair)
    from_far, from_near = lax.optimization_barrier((from_far, from_near))
    result = for_own + from_near + from_far + jnp.where(edge, from_skip.astype(F32), 0.0)
    head_output, grad_tokens = result[0].astype(BF16), result[1].astype(BF16)
    grads = run_finish(k0, last_x, y0, k1, last_y, x1)
    grad_gate, grad_up, grad_down = (part[None] for part in grads)
    return (head_output, grad_tokens, grad_gate, grad_up, grad_down)


def solution(mesh):
    on_square_of_lines = mesh.shape["dp"] == 4 and mesh.shape["expert"] == 8
    return jax.shard_map(
        on_line if on_square_of_lines else on_device,
        mesh=mesh,
        in_specs=(
            P(("dp", "expert"), None),
            P(("dp", "expert"), None),
            P(("dp", "expert"), None),
            P("expert", None, None),
            P("expert", None, None),
            P("expert", None, None),
        ),
        out_specs=(
            P(("dp", "expert"), None),
            P(("dp", "expert"), None),
            P("expert", None, "dp"),
            P("expert", None, "dp"),
            P("expert", "dp", None),
        ),
        check_vma=False,
    )
```
